512 devices in a mesh: outer: 32 (over x, y, core), inner: 16 (over z).
Axes of the slice: x: 4, y: 4, z: 16, core: 2. Of those that a mesh axis runs over, the one named last changes fastest.
Arguments:
- queries: bfloat16 [65536, 2048], P(('outer', 'inner')), may hold values from -6 to 6
- keys: bfloat16 [65536, 2, 2048], P(('outer', 'inner')), may hold values from -6 to 6
- values: bfloat16 [65536, 2, 2048], P(('outer', 'inner')), may hold values from -6 to 6
- beta_logit: float32 [2, 16, 65536], P(None, None, ('outer', 'inner')), may hold values from -1.5 to 11
- gain: float32 [2048], replicated, may hold values from 0.5 to 1.5
Outputs:
- mixed: bfloat16 [65536, 2048], P(('outer', 'inner'))
The draws below stay inside these ranges and needn't reach their ends.
All inputs are finite; a program needn't handle non-finite values.
Results may differ from the reference program's by a relative error of at most 0.0045.
Values sent between devices are 32-bit elements; how exact they have to be, the bound alone decides.
No kernel may reach another device: no remote copies, remote signals or barrier semaphores. Data moves between devices by JAX's collectives and lax.ppermute only.
A program may use at most 64 MiB of HBM per device.

```python
import jax
import jax.numpy as jnp
from jax import lax

HEAD_COUNT = 16
HEAD = 128
TOK_DEV = 128
D = 2048
SEQUENCE_TOKENS = 65536


def draw_beta_logit(key, part):
    key = jax.random.fold_in(key, 7)
    key_collection = jax.random.split(key, 7)
    fast_count = HEAD_COUNT // 2
    slow_lo = 8.8
    order = jax.random.permutation(key_collection[0], HEAD_COUNT)
    fast = (order < fast_count)[None, :, None]
    blocks = SEQUENCE_TOKENS // TOK_DEV
    base = jax.random.uniform(key_collection[1], (1, HEAD_COUNT, 1), jnp.float32, slow_lo, slow_lo + 1.0)
    block_shift = jax.random.uniform(key_collection[2], (1, HEAD_COUNT, blocks), jnp.float32, -0.5, 0.5)
    block_shift = jnp.repeat(block_shift, TOK_DEV, axis=2)
    noise = jax.random.uniform(key_collection[3], (2, HEAD_COUNT, SEQUENCE_TOKENS), jnp.float32, -0.5, 0.5)
    gradual_segment = base + block_shift + noise
    quick = jax.random.uniform(key_collection[4], (2, HEAD_COUNT, SEQUENCE_TOKENS), jnp.float32, -1.5, 1.5)
    starts = jax.random.randint(key_collection[5], (HEAD_COUNT, 3), 0, SEQUENCE_TOKENS - 32)
    positions = jnp.arange(SEQUENCE_TOKENS, dtype=jnp.int32)[None, None, :]
    interior_part = (positions >= starts[:, :, None]) & (positions < starts[:, :, None] + 32)
    rapid_segment = jnp.any(interior_part, axis=1)[None]
    rapid_segment_values = jax.random.uniform(key_collection[6], (2, HEAD_COUNT, SEQUENCE_TOKENS), jnp.float32, -0.5, 0.5)
    gradual_segment = jnp.where(rapid_segment, rapid_segment_values, gradual_segment)
    return jnp.clip(jnp.where(fast, quick, gradual_segment), -1.5, 11.0).astype(jnp.float32)


def level_of(stream_key, extent, cuts, least, largest):
    level, own = 1.0, jax.random.fold_in(stream_key, 6)
    for axis_at, blocks in cuts:
        draws = jnp.exp(jax.random.uniform(jax.random.fold_in(own, axis_at), (blocks,), jnp.float32, least / len(cuts), largest / len(cuts)))
        level = level * jnp.repeat(draws, extent[axis_at] // blocks).reshape([-1 if axis == axis_at else 1 for axis in range(len(extent))])
    return level


def normal_values(stream_key, dims, spread, bound, cuts=(), kind=jnp.bfloat16):
    values = jax.random.normal(stream_key, dims, jnp.float32) * spread
    if len(cuts) > 0:
        values = level_of(stream_key, dims, cuts, -0.22, 0.18) * values
    return jnp.clip(values, min=-bound, max=bound).astype(kind)


def setup_inputs(seed: int = 0) -> dict:
    seeds = jax.random.split(jax.random.key(seed), 6)
    return {
        "queries": normal_values(seeds[0], (SEQUENCE_TOKENS, D), 1.0, 6.0, ((0, 512),)),
        "keys": normal_values(seeds[1], (SEQUENCE_TOKENS, 2, D), 1.0, 6.0, ((0, 512),)),
        "values": normal_values(seeds[2], (SEQUENCE_TOKENS, 2, D), 1.0, 6.0, ((0, 512),)),
        "beta_logit": draw_beta_logit(jax.random.fold_in(seeds[5], 71), 0),
        "gain": jnp.clip(1.0 + 0.1 * jax.random.normal(seeds[4], (D,), jnp.float32), 0.5, 1.5),
    }


HIGH = lax.Precision.HIGHEST

def unit_rows(field):
    return field / jnp.sqrt(lax.optimization_barrier(jnp.sum(field * field, axis=-1, keepdims=True)) + 1e-06)

def block_terms(queries, keys, values, logits):
    count = queries.shape[0]
    heads = logits.shape[1]
    size = queries.shape[1] // heads
    rows = 2 * count
    qf = unit_rows(queries.astype(jnp.float32).reshape(count, heads, size).transpose(1, 0, 2))
    kf = unit_rows(keys.astype(jnp.float32).reshape(count, 2, heads, size).transpose(2, 0, 1, 3).reshape(heads, rows, size))
    vf = values.astype(jnp.float32).reshape(count, 2, heads, size).transpose(2, 0, 1, 3).reshape(heads, rows, size)
    beta = (2.0 * jax.nn.sigmoid(logits)).transpose(1, 2, 0).reshape(heads, rows)
    gram = jnp.einsum('hrd,hsd->hrs', kf, kf, precision=HIGH)
    row_ids = lax.broadcasted_iota(jnp.int32, (rows, rows), 0)
    col_ids = lax.broadcasted_iota(jnp.int32, (rows, rows), 1)
    strict = (row_ids > col_ids)[None]
    eye_rows = jnp.eye(rows, dtype=jnp.float32)[None]
    system = eye_rows + jnp.where(strict, gram * beta[:, None, :], 0.0)
    both = jnp.concatenate([vf, kf], axis=-1)
    solved = lax.linalg.triangular_solve(system, both, left_side=True, lower=True, unit_diagonal=True)
    fresh = solved[..., :size]
    wmat = solved[..., size:]
    kscaled = kf * beta[:, :, None]
    trans = jnp.eye(size, dtype=jnp.float32)[None] - jnp.einsum('hrd,hre->hde', kscaled, wmat, precision=HIGH)
    offset = jnp.einsum('hrd,hre->hde', kscaled, fresh, precision=HIGH)
    scores = jnp.einsum('htd,hsd->hts', qf, kscaled, precision=HIGH)
    tok_ids = lax.broadcasted_iota(jnp.int32, (count, rows), 0)
    virt_ids = lax.broadcasted_iota(jnp.int32, (count, rows), 1)
    scores = jnp.where((virt_ids <= 2 * tok_ids + 1)[None], scores, 0.0)
    local_out = jnp.einsum('hts,hse->hte', scores, fresh, precision=HIGH)
    carried_q = qf - jnp.einsum('hts,hsd->htd', scores, wmat, precision=HIGH)
    return (trans, offset, local_out, carried_q)

def finish(local_out, carried_q, state, gain):
    heads, count, size = local_out.shape
    outs = local_out + jnp.einsum('htd,hde->hte', carried_q, state, precision=HIGH)
    scale = jnp.sqrt(lax.optimization_barrier(jnp.mean(outs * outs, axis=-1, keepdims=True)) + 1e-06)
    normed = outs / scale * gain.reshape(heads, 1, size)
    return normed.transpose(1, 0, 2).reshape(count, heads * size).astype(jnp.bfloat16)

def reference(queries, keys, values, beta_logit, gain):
    blocks = SEQUENCE_TOKENS // TOK_DEV
    q_blocks = queries.reshape(blocks, TOK_DEV, D)
    k_blocks = keys.reshape(blocks, TOK_DEV, 2, D)
    v_blocks = values.reshape(blocks, TOK_DEV, 2, D)
    l_blocks = beta_logit.reshape(2, HEAD_COUNT, blocks, TOK_DEV).transpose(2, 0, 1, 3)

    def advance(state, pieces):
        q_blk, k_blk, v_blk, l_blk = pieces
        trans, offset, local_out, carried_q = block_terms(q_blk, k_blk, v_blk, l_blk)
        result = finish(local_out, carried_q, state, gain)
        state = jnp.einsum('hde,hef->hdf', trans, state, precision=HIGH) + offset
        return (state, result)
    start = jnp.zeros((HEAD_COUNT, HEAD, HEAD), jnp.float32)
    _, mixed = lax.scan(advance, start, (q_blocks, k_blocks, v_blocks, l_blocks))
    return mixed.reshape(SEQUENCE_TOKENS, D)
```

```python
import jax
import jax.numpy as jnp
from jax import lax
from jax.experimental import pallas as pl
from jax.experimental.pallas import tpu as pltpu
from jax.sharding import Mesh, PartitionSpec as P

F32 = jnp.float32
BF16 = jnp.bfloat16
BASE = 16
GROUP = 128 // BASE
EPS = 1e-06
VMEM = 56 * 1024 * 1024


def parts(x):
    hi = x.astype(BF16)
    lo = (x - hi.astype(F32)).astype(BF16)
    return hi, lo


def dot(a, b):
    return jnp.dot(a, b, preferred_element_type=F32)


def dot_nt(a, b):
    return lax.dot_general(a, b, (((1,), (1,)), ((), ())), preferred_element_type=F32)


def left3(x):
    hi, lo = parts(x)
    return jnp.concatenate([hi, lo], axis=1)


def right3(x):
    hi, lo = parts(x)
    row = jnp.concatenate([hi, lo], axis=1)
    return jnp.concatenate([row, row], axis=0)


def mm3(left, right):
    both = dot(left, right)
    half = both.shape[1] // 2
    return both[:, :half] + both[:, half:]


def iota(shape, dim):
    return lax.broadcasted_iota(jnp.int32, shape, dim)


def reciprocal_root(total):
    y = lax.rsqrt(total)
    return y * (1.5 - 0.5 * total * y * y)


def head_cols(h):
    return slice(h * 128, (h + 1) * 128)


def beta_rows_of(logits):
    heads, count = logits.shape[1], logits.shape[2]
    beta2 = 2.0 / (1.0 + jnp.exp(-logits))
    r_of = iota((count, 2 * count), 1)
    t_of = iota((count, 2 * count), 0)
    beta_rows = jnp.zeros((heads, 2 * count), F32)
    for j in range(2):
        pick = (r_of == 2 * t_of + j).astype(BF16)
        rest = beta2[j]
        for _ in range(3):
            piece = rest.astype(BF16)
            rest = rest - piece.astype(F32)
            beta_rows = beta_rows + dot(piece, pick)
    return beta_rows


def unit_keys(kb):
    kf = kb.astype(F32)
    return kf * reciprocal_root(jnp.sum(kf * kf, axis=1, keepdims=True) + EPS)


def solve_right(rhs, inv, cross):
    z2 = mm3(left3(rhs[:, 128:]), right3(inv[128:]))
    z1 = mm3(left3(rhs[:, :128] - mm3(left3(z2), right3(cross))), right3(inv[:128]))
    return jnp.concatenate([z1, z2], axis=1)


def through_rows(z, kb, vb):
    z_hi, z_lo = parts(z)
    k_hi, k_lo = parts(unit_keys(kb))
    both = jnp.concatenate([k_hi, vb], axis=1)
    prod = dot(z_hi, both) + dot(z_lo, both)
    return prod[:, :128] + dot(z_hi, k_lo), prod[:, 128:]


def maps_kernel(k_ref, v_ref, logit_ref, maps_ref, inv_ref, cross_ref, scale_ref, n_ref, r_ref, c_ref):
    rows = k_ref.shape[0]
    size = 128
    beta_rows = beta_rows_of(logit_ref[...])

    row256 = iota((rows, rows), 0)
    col256 = iota((rows, rows), 1)
    strict = row256 > col256
    diagonal = row256 == col256
    row128 = iota((size, size), 0)
    col128 = iota((size, size), 1)
    eye_b = (row128 == col128).astype(BF16)

    compact = [jnp.zeros((BASE, 128), F32) for _ in range(rows // BASE)]
    lane = iota((BASE, 128), 1)
    for h in range(GROUP):
        kb = k_ref[:, head_cols(h)]
        grams = dot_nt(jnp.concatenate([kb, eye_b], axis=0), kb)
        gram = grams[:rows]
        kf = kb.astype(F32)
        n_col = reciprocal_root(jnp.sum(kf * kf, axis=1, keepdims=True) + EPS)
        n_row = reciprocal_root(jnp.sum(jnp.where(diagonal, gram, 0.0), axis=0, keepdims=True) + EPS)
        scale_row = n_row * beta_rows[h : h + 1, :]
        scale_ref[h : h + 1, :] = scale_row
        system = jnp.where(strict, gram, 0.0) * n_col * scale_row
        n_ref[h] = system
        cross_ref[h] = system[size:, :size]
        r_ref[h] = grams[rows:] * scale_row
        mine = (lane // BASE) == h
        for blk in range(rows // BASE):
            place = blk % GROUP
            tile = blk // GROUP
            slab = system[blk * BASE : (blk + 1) * BASE, tile * 128 : (tile + 1) * 128]
            shift = BASE * ((h - place) % GROUP)
            if shift:
                slab = pltpu.roll(slab, shift, axis=1)
            compact[blk] = jnp.where(mine, slab, compact[blk])

    identity = (iota((BASE, 128), 0) == (lane % BASE)).astype(F32)
    for blk in range(rows // BASE):
        below = compact[blk]
        inv = identity
        for step in range(BASE - 1):
            factor = jnp.take_along_axis(below, (lane // BASE) * BASE + step, axis=1, mode="promise_in_bounds")
            inv = inv - factor * inv[step : step + 1, :]
        c_ref[blk] = inv

    eye = (row128 == col128).astype(F32)
    for h in range(GROUP):
        for tile in range(2):
            pieces = []
            for place in range(GROUP):
                slab = c_ref[tile * GROUP + place]
                shift = BASE * ((place - h) % GROUP)
                if shift:
                    slab = pltpu.roll(slab, shift, axis=1)
                pieces.append(jnp.where((lane // BASE) == place, slab, 0.0))
            inv = jnp.concatenate(pieces, axis=0)
            lower = n_ref[h, tile * 128 : (tile + 1) * 128, tile * 128 : (tile + 1) * 128]
            width = BASE
            while width < size:
                mask = (row128 // (2 * width) == col128 // (2 * width)) & (row128 // width != col128 // width)
                part = jnp.where(mask, lower, 0.0)
                inv_right = right3(inv)
                inv = inv - mm3(left3(inv), right3(mm3(left3(part), inv_right)))
                width *= 2
            inv_ref[h, tile * 128 : (tile + 1) * 128] = inv
        z = solve_right(r_ref[h], inv_ref[h], cross_ref[h])
        through, fresh = through_rows(z, k_ref[:, head_cols(h)], v_ref[:, head_cols(h)])
        maps_ref[h, :, :size] = eye - through
        maps_ref[h, :, size:] = fresh


def block_maps(group, keys, values, logits):
    rows, width = keys.shape
    size = 128
    lanes = GROUP * size
    whole = lambda *shape: pl.BlockSpec(shape, lambda g: (0,) * len(shape))
    return pl.pallas_call(
        maps_kernel,
        grid=(1,),
        in_specs=[
            pl.BlockSpec((rows, lanes), lambda g: (0, group)),
            pl.BlockSpec((rows, lanes), lambda g: (0, group)),
            pl.BlockSpec((2, GROUP, rows // 2), lambda g: (0, group, 0)),
        ],
        out_specs=[
            whole(GROUP, size, 2 * size),
            whole(GROUP, rows, size),
            whole(GROUP, size, size),
            whole(GROUP, rows),
        ],
        out_shape=[
            jax.ShapeDtypeStruct((GROUP, size, 2 * size), F32),
            jax.ShapeDtypeStruct((GROUP, rows, size), F32),
            jax.ShapeDtypeStruct((GROUP, size, size), F32),
            jax.ShapeDtypeStruct((GROUP, rows), F32),
        ],
        scratch_shapes=[
            pltpu.VMEM((GROUP, rows, rows), F32),
            pltpu.VMEM((GROUP, size, rows), F32),
            pltpu.VMEM((rows // BASE, BASE, 128), F32),
        ],
        compiler_params=pltpu.CompilerParams(vmem_limit_bytes=VMEM),
        name="block_maps",
    )(keys, values, logits)


def tokens_kernel(q_ref, k_ref, v_ref, inv_ref, cross_ref, scale_ref, lout_ref, cq_ref):
    count = q_ref.shape[0]
    seen = iota((count, 2 * count), 1) <= 2 * iota((count, 2 * count), 0) + 1
    for h in range(GROUP):
        kb = k_ref[:, head_cols(h)]
        qb = q_ref[:, head_cols(h)]
        scores = jnp.where(seen, dot_nt(qb, kb), 0.0) * scale_ref[h : h + 1, :]
        z = solve_right(scores, inv_ref[h], cross_ref[h])
        through, fresh = through_rows(z, kb, v_ref[:, head_cols(h)])
        qf = qb.astype(F32)
        nq = reciprocal_root(jnp.sum(qf * qf, axis=1, keepdims=True) + EPS)
        cq_ref[h] = nq * (qf - through)
        lout_ref[h] = nq * fresh


def block_tokens(group, queries, keys, values, inv, cross, scale):
    count, width = queries.shape
    rows = 2 * count
    size = 128
    lanes = GROUP * size
    whole = lambda *shape: pl.BlockSpec(shape, lambda g: (0,) * len(shape))
    return pl.pallas_call(
        tokens_kernel,
        grid=(1,),
        in_specs=[
            pl.BlockSpec((count, lanes), lambda g: (0, group)),
            pl.BlockSpec((rows, lanes), lambda g: (0, group)),
            pl.BlockSpec((rows, lanes), lambda g: (0, group)),
            whole(GROUP, rows, size),
            whole(GROUP, size, size),
            whole(GROUP, rows),
        ],
        out_specs=[whole(GROUP, count, size), whole(GROUP, count, size)],
        out_shape=[
            jax.ShapeDtypeStruct((GROUP, count, size), F32),
            jax.ShapeDtypeStruct((GROUP, count, size), F32),
        ],
        compiler_params=pltpu.CompilerParams(vmem_limit_bytes=VMEM),
        name="block_tokens",
    )(queries, keys, values, inv, cross, scale)


def times_map(piece, acc):
    left = left3(piece[:, :128])
    hi, lo = parts(acc)
    return dot(left, jnp.concatenate([hi, hi], axis=0)) + dot(left[:, :128], lo)


def after(piece, acc):
    size = piece.shape[0]
    moved = times_map(piece, acc)
    return jnp.concatenate([moved[:, :size], moved[:, size:] + piece[:, size:]], axis=1)


def advance(piece, state):
    return times_map(piece, state) + piece[:, piece.shape[0] :]


def chain_kernel(maps_ref, total_ref):
    for j in range(maps_ref.shape[1]):
        acc = maps_ref[0, j]
        for i in range(1, maps_ref.shape[0]):
            acc = after(maps_ref[i, j], acc)
        total_ref[j] = acc


def chain(maps, name):
    return pl.pallas_call(
        chain_kernel,
        out_shape=jax.ShapeDtypeStruct(maps.shape[1:], F32),
        compiler_params=pltpu.CompilerParams(vmem_limit_bytes=VMEM),
        name=name,
    )(maps)


def start_kernel(place_ref, by_x_ref, by_y_ref, by_core_ref, quads_ref, entry_ref):
    size = by_x_ref.shape[1]
    state = jnp.zeros((size, size), F32)
    for axis, ref in enumerate((by_x_ref, by_y_ref, by_core_ref)):
        state = lax.fori_loop(0, place_ref[axis], lambda i, s, ref=ref: advance(ref[i], s), state)
    entry_ref[0] = state
    for i in range(quads_ref.shape[0] - 1):
        state = advance(quads_ref[i], state)
        entry_ref[i + 1] = state


def start_states(place, by_x, by_y, by_core, quads):
    count, size, _ = quads.shape
    vmem = pl.BlockSpec(memory_space=pltpu.VMEM)
    return pl.pallas_call(
        start_kernel,
        in_specs=[pl.BlockSpec(memory_space=pltpu.SMEM), vmem, vmem, vmem, vmem],
        out_shape=jax.ShapeDtypeStruct((count, size, size), F32),
        compiler_params=pltpu.CompilerParams(vmem_limit_bytes=VMEM),
        name="start_states",
    )(place, by_x, by_y, by_core, quads)


def spread_kernel(start_ref, first_ref, second_ref, entry_ref):
    members, per = first_ref.shape[0], first_ref.shape[1]
    for j in range(start_ref.shape[0]):
        ref = (first_ref, second_ref)[j // per]
        state = start_ref[j]
        entry_ref[0, j] = state
        for i in range(members - 1):
            state = advance(ref[i, j % per], state)
            entry_ref[i + 1, j] = state


def spread(start, first, second):
    heads, size, _ = start.shape
    return pl.pallas_call(
        spread_kernel,
        out_shape=jax.ShapeDtypeStruct((first.shape[0], heads, size, size), F32),
        compiler_params=pltpu.CompilerParams(vmem_limit_bytes=VMEM),
        name="spread",
    )(start, first, second)


def finish_kernel(lout_ref, cq_ref, state_ref, gain_ref, out_ref):
    for h in range(lout_ref.shape[0]):
        outs = lout_ref[h] + mm3(left3(cq_ref[h]), right3(state_ref[h]))
        total = jnp.mean(outs * outs, axis=1, keepdims=True) + EPS
        normed = outs / jnp.sqrt(total) * gain_ref[:, head_cols(h)]
        out_ref[:, head_cols(h)] = normed.astype(BF16)


def finish(tokens, state, gain):
    (lout0, cq0), (lout1, cq1) = tokens
    count, size = lout0.shape[1], lout0.shape[2]
    members, groups, per = state.shape[0], state.shape[1], state.shape[2]
    heads = members * groups * per

    def kernel(l0, c0, l1, c1, state_ref, gain_ref, out_ref):
        pick = pl.program_id(0) < members

        @pl.when(pick)
        def _():
            finish_kernel(l0, c0, state_ref, gain_ref, out_ref)

        @pl.when(jnp.logical_not(pick))
        def _():
            finish_kernel(l1, c1, state_ref, gain_ref, out_ref)

    low = pl.BlockSpec((per, count, size), lambda g: (jnp.minimum(g, members - 1), 0, 0))
    high = pl.BlockSpec((per, count, size), lambda g: (jnp.maximum(g - members, 0), 0, 0))
    return pl.pallas_call(
        kernel,
        grid=(members * groups,),
        in_specs=[
            low,
            low,
            high,
            high,
            pl.BlockSpec((None, None, per, size, size), lambda g: (g % members, g // members, 0, 0, 0)),
            pl.BlockSpec((1, per * size), lambda g: (0, g)),
        ],
        out_specs=pl.BlockSpec((count, per * size), lambda g: (0, g)),
        out_shape=jax.ShapeDtypeStruct((count, heads * size), BF16),
        compiler_params=pltpu.CompilerParams(vmem_limit_bytes=VMEM),
        name="finish",
    )(lout0, cq0, lout1, cq1, state, gain.reshape(1, heads * size))


def local(queries, keys, values, beta_logit, gain):
    count, width = queries.shape
    keys = keys.reshape(2 * count, width)
    values = values.reshape(2 * count, width)
    quad = lax.axis_size("zi")
    size = 128
    received = []
    saved = []
    for group in range(2):
        maps, inv, cross, scale = block_maps(group, keys, values, beta_logit)
        saved.append((inv, cross, scale))
        got = lax.all_to_all(maps, "zi", split_axis=0, concat_axis=0, tiled=True)
        received.append(got.reshape(quad, GROUP // quad, size, 2 * size))
    tokens = [block_tokens(group, queries, keys, values, *saved[group]) for group in range(2)]
    totals = jnp.concatenate([chain(got, "quad_total") for got in received], axis=0)
    quads = lax.all_to_all(totals, "zq", split_axis=0, concat_axis=0, tiled=True)
    whole = chain(quads[:, None], "group_total")
    by_core = lax.all_gather(whole[0], "core")
    by_y = lax.all_gather(chain(by_core[:, None], "chip_total")[0], "y")
    by_x = lax.all_gather(chain(by_y[:, None], "y_total")[0], "x")
    place = jnp.stack([lax.axis_index("x"), lax.axis_index("y"), lax.axis_index("core")])
    starts = start_states(place, by_x, by_y, by_core, quads)
    mine = lax.all_to_all(starts, "zq", split_axis=0, concat_axis=0, tiled=True)
    entries = spread(mine, received[0], received[1])
    state = lax.all_to_all(entries, "zi", split_axis=0, concat_axis=0, tiled=True)
    state = state.reshape(quad, 2, GROUP // quad, size, size)
    return finish(tokens, state, gain)


def solution(mesh):
    fine = Mesh(mesh.devices.reshape(4, 4, 2, 4, 4), ("x", "y", "core", "zq", "zi"))
    every = ("x", "y", "core", "zq", "zi")
    return jax.shard_map(
        local,
        mesh=fine,
        in_specs=(
            P(every, None),
            P(every, None, None),
            P(every, None, None),
            P(None, None, every),
            P(),
        ),
        out_specs=P(every, None),
        check_vma=False,
    )
```

```python
import functools

import jax
import jax.numpy as jnp
from jax import lax
from jax.experimental import pallas as pl
from jax.experimental.pallas import tpu as pltpu
from jax.sharding import Mesh, PartitionSpec as P

F32 = jnp.float32
BF16 = jnp.bfloat16
BASE = 16
GROUP = 128 // BASE
EPS = 1e-06
VMEM = 56 * 1024 * 1024


def parts(x):
    hi = x.astype(BF16)
    lo = (x - hi.astype(F32)).astype(BF16)
    return hi, lo


def dot(a, b):
    return jnp.dot(a, b, preferred_element_type=F32)


def dot_nt(a, b):
    return lax.dot_general(a, b, (((1,), (1,)), ((), ())), preferred_element_type=F32)


def left3(x):
    hi, lo = parts(x)
    return jnp.concatenate([hi, lo], axis=1)


def right3(x):
    hi, lo = parts(x)
    row = jnp.concatenate([hi, lo], axis=1)
    return jnp.concatenate([row, row], axis=0)


def mm3(left, right):
    both = dot(left, right)
    half = both.shape[1] // 2
    return both[:, :half] + both[:, half:]


IN_VMEM = pl.BlockSpec(memory_space=pltpu.VMEM)


def iota(shape, dim):
    return lax.broadcasted_iota(jnp.int32, shape, dim)


def reciprocal_root(total):
    y = lax.rsqrt(total)
    return y * (1.5 - 0.5 * total * y * y)


def head_rows(ref, h):
    return ref[:, :, head_cols(h)].reshape(2 * ref.shape[0], 128)


def head_cols(h):
    return slice(h * 128, (h + 1) * 128)


def beta_rows_of(logits):
    heads, count = logits.shape[1], logits.shape[2]
    beta2 = 2.0 / (1.0 + jnp.exp(-logits))
    r_of = iota((count, 2 * count), 1)
    t_of = iota((count, 2 * count), 0)
    beta_rows = jnp.zeros((heads, 2 * count), F32)
    for j in range(2):
        pick = (r_of == 2 * t_of + j).astype(BF16)
        rest = beta2[j]
        for _ in range(3):
            piece = rest.astype(BF16)
            rest = rest - piece.astype(F32)
            beta_rows = beta_rows + dot(piece, pick)
    return beta_rows


def unit_keys(kb):
    kf = kb.astype(F32)
    return kf * reciprocal_root(jnp.sum(kf * kf, axis=1, keepdims=True) + EPS)


def solve_right(rhs, inv, cross):
    z2 = mm3(left3(rhs[:, 128:]), right3(inv[128:]))
    z1 = mm3(left3(rhs[:, :128] - mm3(left3(z2), right3(cross))), right3(inv[:128]))
    return jnp.concatenate([z1, z2], axis=1)


def through_rows(z, kb, vb):
    z_hi, z_lo = parts(z)
    k_hi, k_lo = parts(unit_keys(kb))
    both = jnp.concatenate([k_hi, vb], axis=1)
    prod = dot(z_hi, both) + dot(z_lo, both)
    return prod[:, :128] + dot(z_hi, k_lo), prod[:, 128:]


def maps_kernel(k_ref, v_ref, logit_ref, maps_ref, inv_ref, cross_ref, scale_ref, n_ref, r_ref, c_ref, t_ref, z_ref):
    rows = 2 * k_ref.shape[0]
    size = 128
    beta_rows = beta_rows_of(logit_ref[...])

    row256 = iota((rows, rows), 0)
    col256 = iota((rows, rows), 1)
    strict = row256 > col256
    diagonal = row256 == col256
    row128 = iota((size, size), 0)
    col128 = iota((size, size), 1)
    eye_b = (row128 == col128).astype(BF16)

    compact = [jnp.zeros((BASE, 128), F32) for _ in range(rows // BASE)]
    lane = iota((BASE, 128), 1)
    for h in range(GROUP):
        kb = head_rows(k_ref, h)
        grams = dot_nt(jnp.concatenate([kb, eye_b], axis=0), kb)
        gram = grams[:rows]
        kf = kb.astype(F32)
        n_col = reciprocal_root(jnp.sum(kf * kf, axis=1, keepdims=True) + EPS)
        n_row = reciprocal_root(jnp.sum(jnp.where(diagonal, gram, 0.0), axis=0, keepdims=True) + EPS)
        scale_row = n_row * beta_rows[h : h + 1, :]
        scale_ref[h : h + 1, :] = scale_row
        system = jnp.where(strict, gram, 0.0) * n_col * scale_row
        n_ref[h] = system
        cross_ref[h] = system[size:, :size]
        r_ref[h] = grams[rows:] * scale_row
        mine = (lane // BASE) == h
        for blk in range(rows // BASE):
            place = blk % GROUP
            tile = blk // GROUP
            slab = system[blk * BASE : (blk + 1) * BASE, tile * 128 : (tile + 1) * 128]
            shift = BASE * ((h - place) % GROUP)
            if shift:
                slab = pltpu.roll(slab, shift, axis=1)
            compact[blk] = jnp.where(mine, slab, compact[blk])

    identity = (iota((BASE, 128), 0) == (lane % BASE)).astype(F32)
    for blk in range(rows // BASE):
        below = compact[blk]
        inv = identity
        for step in range(BASE - 1):
            factor = jnp.take_along_axis(below, (lane // BASE) * BASE + step, axis=1, mode="promise_in_bounds")
            inv = inv - factor * inv[step : step + 1, :]
        c_ref[blk] = inv

    for h in range(GROUP):
        for tile in range(2):
            for place in range(GROUP):
                slab = c_ref[tile * GROUP + place]
                shift = BASE * ((place - h) % GROUP)
                if shift:
                    slab = pltpu.roll(slab, shift, axis=1)
                first = tile * 128 + place * BASE
                inv_ref[h, first : first + BASE] = jnp.where((lane // BASE) == place, slab, 0.0)
    width = BASE
    while width < size:
        odd = range(width, size, 2 * width)
        mask = col128[:width] // width
        for h in range(GROUP):
            for tile in range(2):
                base = tile * 128
                inv = inv_ref[h, base : base + 128]
                part = jnp.concatenate(
                    [
                        jnp.where(mask == at // width - 1, n_ref[h, base + at : base + at + width, base : base + 128], 0.0)
                        for at in odd
                    ],
                    axis=0,
                )
                t_ref[h, tile] = mm3(left3(part), right3(inv))
        for h in range(GROUP):
            for tile in range(2):
                base = tile * 128
                own = jnp.concatenate([inv_ref[h, base + at : base + at + width] for at in odd], axis=0)
                hi, lo = parts(t_ref[h, tile])
                both = jnp.concatenate([hi, lo], axis=1)
                none = jnp.zeros((width, 256), BF16)
                spread = []
                for i in range(len(odd)):
                    spread += [none, both[i * width : (i + 1) * width]]
                spread = jnp.concatenate(spread, axis=0)
                new = own - mm3(left3(own), jnp.concatenate([spread, spread], axis=0))
                for i, at in enumerate(odd):
                    inv_ref[h, base + at : base + at + width] = new[i * width : (i + 1) * width]
        width *= 2

    eye = (row128 == col128).astype(F32)
    for h in range(GROUP):
        z_ref[h, :, size:] = mm3(left3(r_ref[h, :, size:]), right3(inv_ref[h, size:]))
    for h in range(GROUP):
        r_ref[h, :, :size] = r_ref[h, :, :size] - mm3(left3(z_ref[h, :, size:]), right3(cross_ref[h]))
    for h in range(GROUP):
        z_ref[h, :, :size] = mm3(left3(r_ref[h, :, :size]), right3(inv_ref[h, :size]))
    for h in range(GROUP):
        through, fresh = through_rows(z_ref[h], head_rows(k_ref, h), head_rows(v_ref, h))
        maps_ref[h, :, :size] = eye - through
        maps_ref[h, :, size:] = fresh


def block_maps(group, keys, values, logits):
    rows = 2 * keys.shape[0]
    size = 128
    lanes = GROUP * size
    whole = lambda *shape: pl.BlockSpec(shape, lambda g: (0,) * len(shape))
    return pl.pallas_call(
        maps_kernel,
        grid=(1,),
        in_specs=[
            pl.BlockSpec((rows // 2, 2, lanes), lambda g: (0, 0, group)),
            pl.BlockSpec((rows // 2, 2, lanes), lambda g: (0, 0, group)),
            pl.BlockSpec((2, GROUP, rows // 2), lambda g: (0, group, 0)),
        ],
        out_specs=[
            whole(GROUP, size, 2 * size),
            whole(GROUP, rows, size),
            whole(GROUP, size, size),
            whole(GROUP, rows),
        ],
        out_shape=[
            jax.ShapeDtypeStruct((GROUP, size, 2 * size), F32),
            jax.ShapeDtypeStruct((GROUP, rows, size), F32),
            jax.ShapeDtypeStruct((GROUP, size, size), F32),
            jax.ShapeDtypeStruct((GROUP, rows), F32),
        ],
        scratch_shapes=[
            pltpu.VMEM((GROUP, rows, rows), F32),
            pltpu.VMEM((GROUP, size, rows), F32),
            pltpu.VMEM((rows // BASE, BASE, 128), F32),
            pltpu.VMEM((GROUP, 2, size // 2, size), F32),
            pltpu.VMEM((GROUP, size, rows), F32),
        ],
        compiler_params=pltpu.CompilerParams(vmem_limit_bytes=VMEM),
        name="block_maps",
    )(keys, values, logits)


def tokens_kernel(q_ref, k_ref, v_ref, inv_ref, cross_ref, scale_ref, lout_ref, cq_ref):
    count = q_ref.shape[0]
    seen = iota((count, 2 * count), 1) <= 2 * iota((count, 2 * count), 0) + 1
    for h in range(GROUP):
        kb = head_rows(k_ref, h)
        qb = q_ref[:, head_cols(h)]
        scores = jnp.where(seen, dot_nt(qb, kb), 0.0) * scale_ref[h : h + 1, :]
        z = solve_right(scores, inv_ref[h], cross_ref[h])
        through, fresh = through_rows(z, kb, head_rows(v_ref, h))
        qf = qb.astype(F32)
        nq = reciprocal_root(jnp.sum(qf * qf, axis=1, keepdims=True) + EPS)
        cq_ref[h] = nq * (qf - through)
        lout_ref[h] = nq * fresh


def block_tokens(group, queries, keys, values, inv, cross, scale):
    count, width = queries.shape
    rows = 2 * count
    size = 128
    lanes = GROUP * size
    whole = lambda *shape: pl.BlockSpec(shape, lambda g: (0,) * len(shape))
    return pl.pallas_call(
        tokens_kernel,
        grid=(1,),
        in_specs=[
            pl.BlockSpec((count, lanes), lambda g: (0, group)),
            pl.BlockSpec((rows // 2, 2, lanes), lambda g: (0, 0, group)),
            pl.BlockSpec((rows // 2, 2, lanes), lambda g: (0, 0, group)),
            whole(GROUP, rows, size),
            whole(GROUP, size, size),
            whole(GROUP, rows),
        ],
        out_specs=[whole(GROUP, count, size), whole(GROUP, count, size)],
        out_shape=[
            jax.ShapeDtypeStruct((GROUP, count, size), F32),
            jax.ShapeDtypeStruct((GROUP, count, size), F32),
        ],
        compiler_params=pltpu.CompilerParams(vmem_limit_bytes=VMEM),
        name="block_tokens",
    )(queries, keys, values, inv, cross, scale)


def times_map(piece, acc):
    left = left3(piece[:, :128])
    hi, lo = parts(acc)
    return dot(left, jnp.concatenate([hi, hi], axis=0)) + dot(left[:, :128], lo)


def after(piece, acc):
    size = piece.shape[0]
    moved = times_map(piece, acc)
    return jnp.concatenate([moved[:, :size], moved[:, size:] + piece[:, size:]], axis=1)


def advance(piece, state):
    return times_map(piece, state) + piece[:, piece.shape[0] :]


def chain_kernel(pieces, maps_ref, *refs):
    total_ref = refs[-1]
    heads = maps_ref.shape[0] // pieces
    done = 0
    for earlier in refs[:-1]:
        done = earlier.shape[0]
        total_ref[:done] = earlier[...]
    accs = [maps_ref[j] for j in range(heads)]
    for i in range(1, pieces):
        accs = [after(maps_ref[i * heads + j], acc) for j, acc in enumerate(accs)]
    for j, acc in enumerate(accs):
        total_ref[done + j] = acc


def chain(name, pieces, maps, *earlier):
    count = maps.shape[0] // pieces + sum(part.shape[0] for part in earlier)
    return pl.pallas_call(
        functools.partial(chain_kernel, pieces),
        in_specs=[IN_VMEM] * (1 + len(earlier)),
        out_specs=IN_VMEM,
        out_shape=jax.ShapeDtypeStruct((count,) + maps.shape[1:], F32),
        compiler_params=pltpu.CompilerParams(vmem_limit_bytes=VMEM),
        name=name,
    )(maps, *earlier)


def start_kernel(place_ref, by_x_ref, by_y_ref, by_core_ref, quads_ref, entry_ref):
    size = by_x_ref.shape[1]
    state = jnp.zeros((size, size), F32)
    for axis, ref in enumerate((by_x_ref, by_y_ref, by_core_ref)):
        state = lax.fori_loop(0, place_ref[axis], lambda i, s, ref=ref: advance(ref[i], s), state)
    entry_ref[0] = state
    for i in range(quads_ref.shape[0] - 1):
        state = advance(quads_ref[i], state)
        entry_ref[i + 1] = state


def start_states(place, by_x, by_y, by_core, quads):
    count, size, _ = quads.shape
    return pl.pallas_call(
        start_kernel,
        in_specs=[pl.BlockSpec(memory_space=pltpu.SMEM)] + [IN_VMEM] * 4,
        out_specs=IN_VMEM,
        out_shape=jax.ShapeDtypeStruct((count, size, size), F32),
        compiler_params=pltpu.CompilerParams(vmem_limit_bytes=VMEM),
        name="start_states",
    )(place, by_x, by_y, by_core, quads)


def spread_kernel(start_ref, first_ref, second_ref, entry_ref):
    heads = start_ref.shape[0]
    per = heads // 2
    members = first_ref.shape[0] // per
    states = [start_ref[j] for j in range(heads)]
    for i in range(members):
        for j in range(heads):
            entry_ref[i * heads + j] = states[j]
        if i < members - 1:
            states = [advance((first_ref, second_ref)[j // per][i * per + j % per], states[j]) for j in range(heads)]


def spread(start, first, second):
    heads, size, _ = start.shape
    members = 2 * first.shape[0] // heads
    return pl.pallas_call(
        spread_kernel,
        in_specs=[IN_VMEM] * 3,
        out_specs=IN_VMEM,
        out_shape=jax.ShapeDtypeStruct((members * heads, size, size), F32),
        compiler_params=pltpu.CompilerParams(vmem_limit_bytes=VMEM),
        name="spread",
    )(start, first, second)


def finish_kernel(lout_ref, cq_ref, states, gain_ref, out_ref):
    rights = [right3(state) for state in states]
    outs = [lout_ref[h] + mm3(left3(cq_ref[h]), right) for h, right in enumerate(rights)]
    roots = [jnp.sqrt(jnp.mean(out * out, axis=1, keepdims=True) + EPS) for out in outs]
    for h, (out, root) in enumerate(zip(outs, roots)):
        out_ref[:, head_cols(h)] = (out / root * gain_ref[:, head_cols(h)]).astype(BF16)


def finish(tokens, state, gain):
    (lout0, cq0), (lout1, cq1) = tokens
    count, size = lout0.shape[1], lout0.shape[2]
    groups, heads = 2, state.shape[0]
    per = 2
    step_heads = 4
    steps = heads // step_heads
    half = steps // groups

    def kernel(l0, c0, l1, c1, state_ref, gain_ref, out_ref):
        at = pl.program_id(0)

        def run(lout_ref, cq_ref, group):
            first = (at - group * half) * (step_heads // per)
            states = [state_ref[(first + h // per) * groups * per + group * per + h % per] for h in range(step_heads)]
            finish_kernel(lout_ref, cq_ref, states, gain_ref, out_ref)

        @pl.when(at < half)
        def _():
            run(l0, c0, 0)

        @pl.when(at >= half)
        def _():
            run(l1, c1, 1)

    low = pl.BlockSpec((step_heads, count, size), lambda g: (jnp.minimum(g, half - 1), 0, 0))
    high = pl.BlockSpec((step_heads, count, size), lambda g: (jnp.maximum(g - half, 0), 0, 0))
    return pl.pallas_call(
        kernel,
        grid=(steps,),
        in_specs=[
            low,
            low,
            high,
            high,
            IN_VMEM,
            pl.BlockSpec((1, step_heads * size), lambda g: (0, g)),
        ],
        out_specs=pl.BlockSpec((count, step_heads * size), lambda g: (0, g)),
        out_shape=jax.ShapeDtypeStruct((count, heads * size), BF16),
        compiler_params=pltpu.CompilerParams(vmem_limit_bytes=VMEM),
        name="finish",
    )(lout0, cq0, lout1, cq1, state, gain.reshape(1, heads * size))


def local(queries, keys, values, beta_logit, gain):
    quad = lax.axis_size("zi")
    received = []
    saved = []
    for group in range(2):
        maps, inv, cross, scale = block_maps(group, keys, values, beta_logit)
        saved.append((inv, cross, scale))
        got = lax.all_to_all(maps, "zi", split_axis=0, concat_axis=0, tiled=True)
        received.append(got)
    tokens = [block_tokens(group, queries, keys, values, *saved[group]) for group in range(2)]
    totals = chain("quad_total", quad, received[1], chain("quad_total", quad, received[0]))
    quads = lax.all_to_all(totals, "zq", split_axis=0, concat_axis=0, tiled=True)
    whole = chain("group_total", lax.axis_size("zq"), quads)
    by_core = lax.all_gather(whole[0], "core")
    by_y = lax.all_gather(chain("chip_total", lax.axis_size("core"), by_core)[0], "y")
    by_x = lax.all_gather(chain("y_total", lax.axis_size("y"), by_y)[0], "x")
    place = jnp.stack([lax.axis_index("x"), lax.axis_index("y"), lax.axis_index("core")])
    starts = start_states(place, by_x, by_y, by_core, quads)
    mine = lax.all_to_all(starts, "zq", split_axis=0, concat_axis=0, tiled=True)
    entries = spread(mine, received[0], received[1])
    state = lax.all_to_all(entries, "zi", split_axis=0, concat_axis=0, tiled=True)
    return finish(tokens, state, gain)


def solution(mesh):
    fine = Mesh(mesh.devices.reshape(4, 4, 2, 4, 4), ("x", "y", "core", "zq", "zi"))
    every = ("x", "y", "core", "zq", "zi")
    return jax.shard_map(
        local,
        mesh=fine,
        in_specs=(
            P(every, None),
            P(every, None, None),
            P(every, None, None),
            P(None, None, every),
            P(),
        ),
        out_specs=P(every, None),
        check_vma=False,
    )
```

```python
import functools

import jax
import jax.numpy as jnp
from jax import lax
from jax.experimental import pallas as pl
from jax.experimental.pallas import tpu as pltpu
from jax.sharding import Mesh, PartitionSpec as P

F32 = jnp.float32
BF16 = jnp.bfloat16
BASE = 16
GROUP = 128 // BASE
CHUNKS = ((0, 4), (4, 12))
EPS = 1e-06
VMEM = 56 * 1024 * 1024


def parts(x):
    hi = x.astype(BF16)
    lo = (x - hi.astype(F32)).astype(BF16)
    return hi, lo


def dot(a, b):
    return jnp.dot(a, b, preferred_element_type=F32)


def dot_nt(a, b):
    return lax.dot_general(a, b, (((1,), (1,)), ((), ())), preferred_element_type=F32)


def left3(x):
    hi, lo = parts(x)
    return jnp.concatenate([hi, lo], axis=1)


def right3(x):
    hi, lo = parts(x)
    row = jnp.concatenate([hi, lo], axis=1)
    return jnp.concatenate([row, row], axis=0)


def mm3(left, right):
    both = dot(left, right)
    half = both.shape[1] // 2
    return both[:, :half] + both[:, half:]


IN_VMEM = pl.BlockSpec(memory_space=pltpu.VMEM)


def iota(shape, dim):
    return lax.broadcasted_iota(jnp.int32, shape, dim)


def reciprocal_root(total):
    y = lax.rsqrt(total)
    return y * (1.5 - 0.5 * total * y * y)


def head_rows(ref, h):
    return ref[:, :, head_cols(h)].reshape(2 * ref.shape[0], 128)


def head_cols(h):
    return slice(h * 128, (h + 1) * 128)


def beta_rows_of(logits):
    heads, count = logits.shape[1], logits.shape[2]
    beta2 = 2.0 / (1.0 + jnp.exp(-logits))
    r_of = iota((count, 2 * count), 1)
    t_of = iota((count, 2 * count), 0)
    beta_rows = jnp.zeros((heads, 2 * count), F32)
    for j in range(2):
        pick = (r_of == 2 * t_of + j).astype(BF16)
        rest = beta2[j]
        for _ in range(3):
            piece = rest.astype(BF16)
            rest = rest - piece.astype(F32)
            beta_rows = beta_rows + dot(piece, pick)
    return beta_rows


def unit_keys(kb):
    kf = kb.astype(F32)
    return kf * reciprocal_root(jnp.sum(kf * kf, axis=1, keepdims=True) + EPS)


def solve_right(rhs, inv, cross):
    z2 = mm3(left3(rhs[:, 128:]), right3(inv[128:]))
    z1 = mm3(left3(rhs[:, :128] - mm3(left3(z2), right3(cross))), right3(inv[:128]))
    return jnp.concatenate([z1, z2], axis=1)


def through_rows(z, kb, vb):
    z_hi, z_lo = parts(z)
    k_hi, k_lo = parts(unit_keys(kb))
    both = jnp.concatenate([k_hi, vb], axis=1)
    prod = dot(z_hi, both) + dot(z_lo, both)
    return prod[:, :128] + dot(z_hi, k_lo), prod[:, 128:]


def maps_kernel(first, heads, skip, k_ref, v_ref, logit_ref, maps_ref, inv_ref, cross_ref, scale_ref, n_ref, r_ref, c_ref, t_ref, z_ref):
    rows = 2 * k_ref.shape[0]
    size = 128
    beta_rows = beta_rows_of(logit_ref[...])

    row256 = iota((rows, rows), 0)
    col256 = iota((rows, rows), 1)
    strict = row256 > col256
    diagonal = row256 == col256
    row128 = iota((size, size), 0)
    col128 = iota((size, size), 1)
    eye_b = (row128 == col128).astype(BF16)

    packs = -(-heads // GROUP)
    compact = [jnp.zeros((BASE, 128), F32) for _ in range(packs * (rows // BASE))]
    lane = iota((BASE, 128), 1)
    for h in range(heads):
        kb = head_rows(k_ref, skip + h)
        grams = dot_nt(jnp.concatenate([kb, eye_b], axis=0), kb)
        gram = grams[:rows]
        kf = kb.astype(F32)
        n_col = reciprocal_root(jnp.sum(kf * kf, axis=1, keepdims=True) + EPS)
        n_row = reciprocal_root(jnp.sum(jnp.where(diagonal, gram, 0.0), axis=0, keepdims=True) + EPS)
        scale_row = n_row * beta_rows[first + h : first + h + 1, :]
        scale_ref[h : h + 1, :] = scale_row
        system = jnp.where(strict, gram, 0.0) * n_col * scale_row
        n_ref[h] = system
        cross_ref[h] = system[size:, :size]
        r_ref[h] = grams[rows:] * scale_row
        slot = h % GROUP
        mine = (lane // BASE) == slot
        for blk in range(rows // BASE):
            place = blk % GROUP
            tile = blk // GROUP
            slab = system[blk * BASE : (blk + 1) * BASE, tile * 128 : (tile + 1) * 128]
            shift = BASE * ((slot - place) % GROUP)
            if shift:
                slab = pltpu.roll(slab, shift, axis=1)
            at = (h // GROUP) * (rows // BASE) + blk
            compact[at] = jnp.where(mine, slab, compact[at])

    identity = (iota((BASE, 128), 0) == (lane % BASE)).astype(F32)
    for blk in range(packs * (rows // BASE)):
        below = compact[blk]
        inv = identity
        for step in range(BASE - 1):
            factor = jnp.take_along_axis(below, (lane // BASE) * BASE + step, axis=1, mode="promise_in_bounds")
            inv = inv - factor * inv[step : step + 1, :]
        c_ref[blk] = inv

    for h in range(heads):
        for tile in range(2):
            for place in range(GROUP):
                slab = c_ref[(h // GROUP) * (rows // BASE) + tile * GROUP + place]
                shift = BASE * ((place - h % GROUP) % GROUP)
                if shift:
                    slab = pltpu.roll(slab, shift, axis=1)
                first = tile * 128 + place * BASE
                inv_ref[h, first : first + BASE] = jnp.where((lane // BASE) == place, slab, 0.0)
    width = BASE
    while width < size:
        odd = range(width, size, 2 * width)
        mask = col128[:width] // width
        for h in range(heads):
            for tile in range(2):
                base = tile * 128
                inv = inv_ref[h, base : base + 128]
                part = jnp.concatenate(
                    [
                        jnp.where(mask == at // width - 1, n_ref[h, base + at : base + at + width, base : base + 128], 0.0)
                        for at in odd
                    ],
                    axis=0,
                )
                t_ref[h, tile] = mm3(left3(part), right3(inv))
        for h in range(heads):
            for tile in range(2):
                base = tile * 128
                own = jnp.concatenate([inv_ref[h, base + at : base + at + width] for at in odd], axis=0)
                hi, lo = parts(t_ref[h, tile])
                both = jnp.concatenate([hi, lo], axis=1)
                none = jnp.zeros((width, 256), BF16)
                spread = []
                for i in range(len(odd)):
                    spread += [none, both[i * width : (i + 1) * width]]
                spread = jnp.concatenate(spread, axis=0)
                new = own - mm3(left3(own), jnp.concatenate([spread, spread], axis=0))
                for i, at in enumerate(odd):
                    inv_ref[h, base + at : base + at + width] = new[i * width : (i + 1) * width]
        width *= 2

    eye = (row128 == col128).astype(F32)
    for h in range(heads):
        z_ref[h, :, size:] = mm3(left3(r_ref[h, :, size:]), right3(inv_ref[h, size:]))
    for h in range(heads):
        r_ref[h, :, :size] = r_ref[h, :, :size] - mm3(left3(z_ref[h, :, size:]), right3(cross_ref[h]))
    for h in range(heads):
        z_ref[h, :, :size] = mm3(left3(r_ref[h, :, :size]), right3(inv_ref[h, :size]))
    for h in range(heads):
        through, fresh = through_rows(z_ref[h], head_rows(k_ref, skip + h), head_rows(v_ref, skip + h))
        maps_ref[h, :, :size] = eye - through
        maps_ref[h, :, size:] = fresh


def whole(*shape):
    return pl.BlockSpec(shape, lambda g: (0,) * len(shape))


def block_maps(chunk, keys, values, logits):
    first, heads = chunk
    rows = 2 * keys.shape[0]
    size = 128
    lanes = heads * size if first == 0 else keys.shape[2]
    return pl.pallas_call(
        functools.partial(maps_kernel, first, heads, first),
        grid=(1,),
        in_specs=[
            whole(rows // 2, 2, lanes),
            whole(rows // 2, 2, lanes),
            whole(*logits.shape),
        ],
        out_specs=[
            whole(heads, size, 2 * size),
            whole(heads, rows, size),
            whole(heads, size, size),
            whole(heads, rows),
        ],
        out_shape=[
            jax.ShapeDtypeStruct((heads, size, 2 * size), F32),
            jax.ShapeDtypeStruct((heads, rows, size), F32),
            jax.ShapeDtypeStruct((heads, size, size), F32),
            jax.ShapeDtypeStruct((heads, rows), F32),
        ],
        scratch_shapes=[
            pltpu.VMEM((heads, rows, rows), F32),
            pltpu.VMEM((heads, size, rows), F32),
            pltpu.VMEM((-(-heads // GROUP) * (rows // BASE), BASE, 128), F32),
            pltpu.VMEM((heads, 2, size // 2, size), F32),
            pltpu.VMEM((heads, size, rows), F32),
        ],
        compiler_params=pltpu.CompilerParams(vmem_limit_bytes=VMEM),
        name="block_maps",
    )(keys, values, logits)


def tokens_kernel(skip, q_ref, k_ref, v_ref, inv_ref, cross_ref, scale_ref, lout_ref, cq_ref):
    count = q_ref.shape[0]
    seen = iota((count, 2 * count), 1) <= 2 * iota((count, 2 * count), 0) + 1
    for h in range(lout_ref.shape[0]):
        kb = head_rows(k_ref, skip + h)
        qb = q_ref[:, head_cols(skip + h)]
        scores = jnp.where(seen, dot_nt(qb, kb), 0.0) * scale_ref[h : h + 1, :]
        z = solve_right(scores, inv_ref[h], cross_ref[h])
        through, fresh = through_rows(z, kb, head_rows(v_ref, skip + h))
        qf = qb.astype(F32)
        nq = reciprocal_root(jnp.sum(qf * qf, axis=1, keepdims=True) + EPS)
        cq_ref[h] = nq * (qf - through)
        lout_ref[h] = nq * fresh


def block_tokens(chunk, queries, keys, values, inv, cross, scale):
    first, heads = chunk
    count = queries.shape[0]
    rows = 2 * count
    size = 128
    lanes = heads * size if first == 0 else queries.shape[1]
    return pl.pallas_call(
        functools.partial(tokens_kernel, first),
        grid=(1,),
        in_specs=[
            whole(count, lanes),
            whole(rows // 2, 2, lanes),
            whole(rows // 2, 2, lanes),
            whole(heads, rows, size),
            whole(heads, size, size),
            whole(heads, rows),
        ],
        out_specs=[whole(heads, count, size), whole(heads, count, size)],
        out_shape=[
            jax.ShapeDtypeStruct((heads, count, size), F32),
            jax.ShapeDtypeStruct((heads, count, size), F32),
        ],
        compiler_params=pltpu.CompilerParams(vmem_limit_bytes=VMEM),
        name="block_tokens",
    )(queries, keys, values, inv, cross, scale)


def times_map(piece, acc):
    left = left3(piece[:, :128])
    hi, lo = parts(acc)
    return dot(left, jnp.concatenate([hi, hi], axis=0)) + dot(left[:, :128], lo)


def after(piece, acc):
    size = piece.shape[0]
    moved = times_map(piece, acc)
    return jnp.concatenate([moved[:, :size], moved[:, size:] + piece[:, size:]], axis=1)


def advance(piece, state):
    return times_map(piece, state) + piece[:, piece.shape[0] :]


def chain_kernel(pieces, maps_ref, *refs):
    total_ref = refs[-1]
    heads = maps_ref.shape[0] // pieces
    done = 0
    for earlier in refs[:-1]:
        done = earlier.shape[0]
        total_ref[:done] = earlier[...]
    accs = [maps_ref[j] for j in range(heads)]
    for i in range(1, pieces):
        accs = [after(maps_ref[i * heads + j], acc) for j, acc in enumerate(accs)]
    for j, acc in enumerate(accs):
        total_ref[done + j] = acc


def chain(name, pieces, maps, *earlier):
    count = maps.shape[0] // pieces + sum(part.shape[0] for part in earlier)
    return pl.pallas_call(
        functools.partial(chain_kernel, pieces),
        in_specs=[IN_VMEM] * (1 + len(earlier)),
        out_specs=IN_VMEM,
        out_shape=jax.ShapeDtypeStruct((count,) + maps.shape[1:], F32),
        compiler_params=pltpu.CompilerParams(vmem_limit_bytes=VMEM),
        name=name,
    )(maps, *earlier)


def start_kernel(place_ref, by_x_ref, by_y_ref, by_core_ref, quads_ref, entry_ref):
    size = by_x_ref.shape[1]
    state = jnp.zeros((size, size), F32)
    for axis, ref in enumerate((by_x_ref, by_y_ref, by_core_ref)):
        state = lax.fori_loop(0, place_ref[axis], lambda i, s, ref=ref: advance(ref[i], s), state)
    entry_ref[0] = state
    for i in range(quads_ref.shape[0] - 1):
        state = advance(quads_ref[i], state)
        entry_ref[i + 1] = state


def start_states(place, by_x, by_y, by_core, quads):
    count, size, _ = quads.shape
    return pl.pallas_call(
        start_kernel,
        in_specs=[pl.BlockSpec(memory_space=pltpu.SMEM)] + [IN_VMEM] * 4,
        out_specs=IN_VMEM,
        out_shape=jax.ShapeDtypeStruct((count, size, size), F32),
        compiler_params=pltpu.CompilerParams(vmem_limit_bytes=VMEM),
        name="start_states",
    )(place, by_x, by_y, by_core, quads)


def spread_kernel(start_ref, first_ref, second_ref, entry_ref):
    heads = start_ref.shape[0]
    members = entry_ref.shape[0] // heads
    early = first_ref.shape[0] // members
    late = heads - early
    states = [start_ref[j] for j in range(heads)]
    for i in range(members):
        for j in range(heads):
            entry_ref[i * heads + j] = states[j]
        if i < members - 1:
            pieces = [first_ref[i * early + j] for j in range(early)] + [second_ref[i * late + j] for j in range(late)]
            states = [advance(piece, state) for piece, state in zip(pieces, states)]


def spread(start, first, second):
    heads, size, _ = start.shape
    members = (first.shape[0] + second.shape[0]) // heads
    return pl.pallas_call(
        spread_kernel,
        in_specs=[IN_VMEM] * 3,
        out_specs=IN_VMEM,
        out_shape=jax.ShapeDtypeStruct((members * heads, size, size), F32),
        compiler_params=pltpu.CompilerParams(vmem_limit_bytes=VMEM),
        name="spread",
    )(start, first, second)


def finish_kernel(lout_ref, cq_ref, states, gain_ref, out_ref):
    rights = [right3(state) for state in states]
    outs = [lout_ref[h] + mm3(left3(cq_ref[h]), right) for h, right in enumerate(rights)]
    roots = [jnp.sqrt(jnp.mean(out * out, axis=1, keepdims=True) + EPS) for out in outs]
    for h, (out, root) in enumerate(zip(outs, roots)):
        out_ref[:, head_cols(h)] = (out / root * gain_ref[:, head_cols(h)]).astype(BF16)


def finish(tokens, state, gain):
    (lout0, cq0), (lout1, cq1) = tokens
    count, size = lout0.shape[1], lout0.shape[2]
    heads = state.shape[0]
    early = lout0.shape[0]
    held = heads // early
    late = held - 1

    def kernel(l0, c0, l1, c1, state_ref, gain_ref, out_ref):
        at = pl.program_id(0)

        @pl.when(at == 0)
        def _():
            states = [state_ref[held * m] for m in range(early)]
            finish_kernel(l0, c0, states, gain_ref, out_ref)

        @pl.when(at > 0)
        def _():
            states = []
            for h in range(early):
                place = (at - 1) * early + h
                member = lax.div(place, late)
                states.append(state_ref[held * member + 1 + place - late * member])
            finish_kernel(l1, c1, states, gain_ref, out_ref)

    low = pl.BlockSpec((early, count, size), lambda g: (0, 0, 0))
    high = pl.BlockSpec((early, count, size), lambda g: (jnp.maximum(g - 1, 0), 0, 0))
    return pl.pallas_call(
        kernel,
        grid=(heads // early,),
        in_specs=[low, low, high, high, IN_VMEM, pl.BlockSpec((1, early * size), lambda g: (0, g))],
        out_specs=pl.BlockSpec((count, early * size), lambda g: (0, g)),
        out_shape=jax.ShapeDtypeStruct((count, heads * size), BF16),
        compiler_params=pltpu.CompilerParams(vmem_limit_bytes=VMEM),
        name="finish",
    )(lout0, cq0, lout1, cq1, state, gain.reshape(1, heads * size))


def local(queries, keys, values, beta_logit, gain):
    quad = lax.axis_size("zi")
    received = []
    saved = []
    for chunk in CHUNKS:
        maps, inv, cross, scale = block_maps(chunk, keys, values, beta_logit)
        saved.append((inv, cross, scale))
        got = lax.all_to_all(maps, "zi", split_axis=0, concat_axis=0, tiled=True)
        received.append(got)
    tokens = [block_tokens(chunk, queries, keys, values, *kept) for chunk, kept in zip(CHUNKS, saved)]
    totals = chain("quad_total", quad, received[1], chain("quad_total", quad, received[0]))
    quads = lax.all_to_all(totals, "zq", split_axis=0, concat_axis=0, tiled=True)
    whole = chain("group_total", lax.axis_size("zq"), quads)
    by_core = lax.all_gather(whole[0], "core")
    by_y = lax.all_gather(chain("chip_total", lax.axis_size("core"), by_core)[0], "y")
    by_x = lax.all_gather(chain("y_total", lax.axis_size("y"), by_y)[0], "x")
    place = jnp.stack([lax.axis_index("x"), lax.axis_index("y"), lax.axis_index("core")])
    starts = start_states(place, by_x, by_y, by_core, quads)
    mine = lax.all_to_all(starts, "zq", split_axis=0, concat_axis=0, tiled=True)
    entries = spread(mine, received[0], received[1])
    state = lax.all_to_all(entries, "zi", split_axis=0, concat_axis=0, tiled=True)
    return finish(tokens, state, gain)


def solution(mesh):
    fine = Mesh(mesh.devices.reshape(4, 4, 2, 4, 4), ("x", "y", "core", "zq", "zi"))
    every = ("x", "y", "core", "zq", "zi")
    return jax.shard_map(
        local,
        mesh=fine,
        in_specs=(
            P(every, None),
            P(every, None, None),
            P(every, None, None),
            P(None, None, every),
            P(),
        ),
        out_specs=P(every, None),
        check_vma=False,
    )
```

```python
import functools

import jax
import jax.numpy as jnp
from jax import lax
from jax.experimental import pallas as pl
from jax.experimental.pallas import tpu as pltpu
from jax.sharding import Mesh, PartitionSpec as P

F32 = jnp.float32
BF16 = jnp.bfloat16
BASE = 16
GROUP = 128 // BASE
EPS = 1e-06
VMEM = 58 * 1024 * 1024
SMALL = 16 * 1024 * 1024


def parts(x):
    hi = x.astype(BF16)
    lo = (x - hi.astype(F32)).astype(BF16)
    return hi, lo


def dot(a, b):
    return jnp.dot(a, b, preferred_element_type=F32)


def dot_nt(a, b):
    return lax.dot_general(a, b, (((1,), (1,)), ((), ())), preferred_element_type=F32)


def left3(x):
    hi, lo = parts(x)
    return jnp.concatenate([hi, lo], axis=1)


def right3(x):
    hi, lo = parts(x)
    row = jnp.concatenate([hi, lo], axis=1)
    return jnp.concatenate([row, row], axis=0)


def mm3(left, right):
    both = dot(left, right)
    half = both.shape[1] // 2
    return both[:, :half] + both[:, half:]


IN_VMEM = pl.BlockSpec(memory_space=pltpu.VMEM)


def held_in_vmem(*arrays):
    return [pltpu.with_memory_space_constraint(array, pltpu.VMEM) for array in arrays]


def iota(shape, dim):
    return lax.broadcasted_iota(jnp.int32, shape, dim)


def reciprocal_root(total):
    y = lax.rsqrt(total)
    return y * (1.5 - 0.5 * total * y * y)


def head_rows(ref, h):
    return ref[:, :, head_cols(h)].reshape(2 * ref.shape[0], 128)


def head_cols(h):
    return slice(h * 128, (h + 1) * 128)


def beta_rows_of(logits):
    heads, count = logits.shape[1], logits.shape[2]
    beta2 = 2.0 / (1.0 + jnp.exp(-logits))
    r_of = iota((count, 2 * count), 1)
    t_of = iota((count, 2 * count), 0)
    beta_rows = jnp.zeros((heads, 2 * count), F32)
    for j in range(2):
        pick = (r_of == 2 * t_of + j).astype(BF16)
        rest = beta2[j]
        for _ in range(3):
            piece = rest.astype(BF16)
            rest = rest - piece.astype(F32)
            beta_rows = beta_rows + dot(piece, pick)
    return beta_rows


def unit_keys(kb):
    kf = kb.astype(F32)
    return kf * reciprocal_root(jnp.sum(kf * kf, axis=1, keepdims=True) + EPS)


def solve_right(rhs, inv, cross):
    z2 = mm3(left3(rhs[:, 128:]), right3(inv[128:]))
    z1 = mm3(left3(rhs[:, :128] - mm3(left3(z2), right3(cross))), right3(inv[:128]))
    return jnp.concatenate([z1, z2], axis=1)


def through_rows(z, kb, vb):
    z_hi, z_lo = parts(z)
    k_hi, k_lo = parts(unit_keys(kb))
    both = jnp.concatenate([k_hi, vb], axis=1)
    prod = dot(z_hi, both) + dot(z_lo, both)
    return prod[:, :128] + dot(z_hi, k_lo), prod[:, 128:]


def maps_kernel(k_ref, v_ref, logit_ref, maps_ref, inv_ref, cross_ref, scale_ref, n_ref, r_ref, c_ref, t_ref, z_ref):
    rows = 2 * k_ref.shape[0]
    size = 128
    beta_rows = beta_rows_of(logit_ref[...])

    row256 = iota((rows, rows), 0)
    col256 = iota((rows, rows), 1)
    strict = row256 > col256
    diagonal = row256 == col256
    row128 = iota((size, size), 0)
    col128 = iota((size, size), 1)
    eye_b = (row128 == col128).astype(BF16)

    compact = [jnp.zeros((BASE, 128), F32) for _ in range(rows // BASE)]
    lane = iota((BASE, 128), 1)
    for h in range(GROUP):
        kb = head_rows(k_ref, h)
        grams = dot_nt(jnp.concatenate([kb, eye_b], axis=0), kb)
        gram = grams[:rows]
        kf = kb.astype(F32)
        n_col = reciprocal_root(jnp.sum(kf * kf, axis=1, keepdims=True) + EPS)
        n_row = reciprocal_root(jnp.sum(jnp.where(diagonal, gram, 0.0), axis=0, keepdims=True) + EPS)
        scale_row = n_row * beta_rows[h : h + 1, :]
        scale_ref[h : h + 1, :] = scale_row
        system = jnp.where(strict, gram, 0.0) * n_col * scale_row
        n_ref[h] = system
        cross_ref[h] = system[size:, :size]
        r_ref[h] = grams[rows:] * scale_row
        mine = (lane // BASE) == h
        for blk in range(rows // BASE):
            place = blk % GROUP
            tile = blk // GROUP
            slab = system[blk * BASE : (blk + 1) * BASE, tile * 128 : (tile + 1) * 128]
            shift = BASE * ((h - place) % GROUP)
            if shift:
                slab = pltpu.roll(slab, shift, axis=1)
            compact[blk] = jnp.where(mine, slab, compact[blk])

    identity = (iota((BASE, 128), 0) == (lane % BASE)).astype(F32)
    for blk in range(rows // BASE):
        below = compact[blk]
        inv = identity
        for step in range(BASE - 1):
            factor = jnp.take_along_axis(below, (lane // BASE) * BASE + step, axis=1, mode="promise_in_bounds")
            inv = inv - factor * inv[step : step + 1, :]
        c_ref[blk] = inv

    for h in range(GROUP):
        for tile in range(2):
            for place in range(GROUP):
                slab = c_ref[tile * GROUP + place]
                shift = BASE * ((place - h) % GROUP)
                if shift:
                    slab = pltpu.roll(slab, shift, axis=1)
                first = tile * 128 + place * BASE
                inv_ref[h, first : first + BASE] = jnp.where((lane // BASE) == place, slab, 0.0)
    width = BASE
    while width < size:
        odd = range(width, size, 2 * width)
        mask = col128[:width] // width
        for h in range(GROUP):
            for tile in range(2):
                base = tile * 128
                inv = inv_ref[h, base : base + 128]
                part = jnp.concatenate(
                    [
                        jnp.where(mask == at // width - 1, n_ref[h, base + at : base + at + width, base : base + 128], 0.0)
                        for at in odd
                    ],
                    axis=0,
                )
                t_ref[h, tile] = mm3(left3(part), right3(inv))
        for h in range(GROUP):
            for tile in range(2):
                base = tile * 128
                own = jnp.concatenate([inv_ref[h, base + at : base + at + width] for at in odd], axis=0)
                hi, lo = parts(t_ref[h, tile])
                both = jnp.concatenate([hi, lo], axis=1)
                none = jnp.zeros((width, 256), BF16)
                spread = []
                for i in range(len(odd)):
                    spread += [none, both[i * width : (i + 1) * width]]
                spread = jnp.concatenate(spread, axis=0)
                new = own - mm3(left3(own), jnp.concatenate([spread, spread], axis=0))
                for i, at in enumerate(odd):
                    inv_ref[h, base + at : base + at + width] = new[i * width : (i + 1) * width]
        width *= 2

    eye = (row128 == col128).astype(F32)
    for h in range(GROUP):
        z_ref[h, :, size:] = mm3(left3(r_ref[h, :, size:]), right3(inv_ref[h, size:]))
    for h in range(GROUP):
        r_ref[h, :, :size] = r_ref[h, :, :size] - mm3(left3(z_ref[h, :, size:]), right3(cross_ref[h]))
    for h in range(GROUP):
        z_ref[h, :, :size] = mm3(left3(r_ref[h, :, :size]), right3(inv_ref[h, :size]))
    for h in range(GROUP):
        through, fresh = through_rows(z_ref[h], head_rows(k_ref, h), head_rows(v_ref, h))
        maps_ref[h, :, :size] = eye - through
        maps_ref[h, :, size:] = fresh


def block_maps(group, keys, values, logits):
    rows = 2 * keys.shape[0]
    size = 128
    lanes = GROUP * size
    whole = lambda *shape: pl.BlockSpec(shape, lambda g: (0,) * len(shape))
    return pl.pallas_call(
        maps_kernel,
        grid=(1,),
        in_specs=[
            pl.BlockSpec((rows // 2, 2, lanes), lambda g: (0, 0, group)),
            pl.BlockSpec((rows // 2, 2, lanes), lambda g: (0, 0, group)),
            pl.BlockSpec((2, GROUP, rows // 2), lambda g: (0, group, 0)),
        ],
        out_specs=[
            whole(GROUP, size, 2 * size),
            whole(GROUP, rows, size),
            whole(GROUP, size, size),
            whole(GROUP, rows),
        ],
        out_shape=[
            jax.ShapeDtypeStruct((GROUP, size, 2 * size), F32),
            jax.ShapeDtypeStruct((GROUP, rows, size), F32),
            jax.ShapeDtypeStruct((GROUP, size, size), F32),
            jax.ShapeDtypeStruct((GROUP, rows), F32),
        ],
        scratch_shapes=[
            pltpu.VMEM((GROUP, rows, rows), F32),
            pltpu.VMEM((GROUP, size, rows), F32),
            pltpu.VMEM((rows // BASE, BASE, 128), F32),
            pltpu.VMEM((GROUP, 2, size // 2, size), F32),
            pltpu.VMEM((GROUP, size, rows), F32),
        ],
        compiler_params=pltpu.CompilerParams(vmem_limit_bytes=VMEM),
        name="block_maps",
    )(keys, values, logits)


def tokens_kernel(q_ref, k_ref, v_ref, inv_ref, cross_ref, scale_ref, lout_ref, cq_ref):
    count = q_ref.shape[0]
    seen = iota((count, 2 * count), 1) <= 2 * iota((count, 2 * count), 0) + 1
    for h in range(GROUP):
        kb = head_rows(k_ref, h)
        qb = q_ref[:, head_cols(h)]
        scores = jnp.where(seen, dot_nt(qb, kb), 0.0) * scale_ref[h : h + 1, :]
        z = solve_right(scores, inv_ref[h], cross_ref[h])
        through, fresh = through_rows(z, kb, head_rows(v_ref, h))
        qf = qb.astype(F32)
        nq = reciprocal_root(jnp.sum(qf * qf, axis=1, keepdims=True) + EPS)
        cq_ref[h] = nq * (qf - through)
        lout_ref[h] = nq * fresh


def block_tokens(group, queries, keys, values, inv, cross, scale):
    count, width = queries.shape
    rows = 2 * count
    size = 128
    lanes = GROUP * size
    whole = lambda *shape: pl.BlockSpec(shape, lambda g: (0,) * len(shape))
    return pl.pallas_call(
        tokens_kernel,
        grid=(1,),
        in_specs=[
            pl.BlockSpec((count, lanes), lambda g: (0, group)),
            pl.BlockSpec((rows // 2, 2, lanes), lambda g: (0, 0, group)),
            pl.BlockSpec((rows // 2, 2, lanes), lambda g: (0, 0, group)),
            whole(GROUP, rows, size),
            whole(GROUP, size, size),
            whole(GROUP, rows),
        ],
        out_specs=[whole(GROUP, count, size), whole(GROUP, count, size)],
        out_shape=[
            jax.ShapeDtypeStruct((GROUP, count, size), F32),
            jax.ShapeDtypeStruct((GROUP, count, size), F32),
        ],
        compiler_params=pltpu.CompilerParams(vmem_limit_bytes=VMEM),
        name="block_tokens",
    )(queries, keys, values, inv, cross, scale)


def times_map(piece, acc):
    left = left3(piece[:, :128])
    hi, lo = parts(acc)
    return dot(left, jnp.concatenate([hi, hi], axis=0)) + dot(left[:, :128], lo)


def after(piece, acc):
    size = piece.shape[0]
    moved = times_map(piece, acc)
    return jnp.concatenate([moved[:, :size], moved[:, size:] + piece[:, size:]], axis=1)


def advance(piece, state):
    return times_map(piece, state) + piece[:, piece.shape[0] :]


def chain_kernel(pieces, maps_ref, *refs):
    total_ref = refs[-1]
    heads = maps_ref.shape[0] // pieces
    done = 0
    for earlier in refs[:-1]:
        done = earlier.shape[0]
        total_ref[:done] = earlier[...]
    accs = [maps_ref[j] for j in range(heads)]
    for i in range(1, pieces):
        accs = [after(maps_ref[i * heads + j], acc) for j, acc in enumerate(accs)]
    for j, acc in enumerate(accs):
        total_ref[done + j] = acc


def chain(name, pieces, maps, *earlier):
    count = maps.shape[0] // pieces + sum(part.shape[0] for part in earlier)
    return pl.pallas_call(
        functools.partial(chain_kernel, pieces),
        in_specs=[IN_VMEM] * (1 + len(earlier)),
        out_specs=IN_VMEM,
        out_shape=jax.ShapeDtypeStruct((count,) + maps.shape[1:], F32),
        compiler_params=pltpu.CompilerParams(vmem_limit_bytes=SMALL),
        name=name,
    )(*held_in_vmem(maps, *earlier))


def start_kernel(place_ref, by_x_ref, by_y_ref, by_core_ref, quads_ref, entry_ref):
    size = by_x_ref.shape[1]
    state = jnp.zeros((size, size), F32)
    for axis, ref in enumerate((by_x_ref, by_y_ref, by_core_ref)):
        state = lax.fori_loop(0, place_ref[axis], lambda i, s, ref=ref: advance(ref[i], s), state)
    entry_ref[0] = state
    for i in range(quads_ref.shape[0] - 1):
        state = advance(quads_ref[i], state)
        entry_ref[i + 1] = state


def start_states(place, by_x, by_y, by_core, quads):
    count, size, _ = quads.shape
    return pl.pallas_call(
        start_kernel,
        in_specs=[pl.BlockSpec(memory_space=pltpu.SMEM)] + [IN_VMEM] * 4,
        out_specs=IN_VMEM,
        out_shape=jax.ShapeDtypeStruct((count, size, size), F32),
        compiler_params=pltpu.CompilerParams(vmem_limit_bytes=SMALL),
        name="start_states",
    )(place, *held_in_vmem(by_x, by_y, by_core, quads))


def spread_kernel(start_ref, first_ref, second_ref, entry_ref):
    heads = start_ref.shape[0]
    per = heads // 2
    members = first_ref.shape[0] // per
    states = [start_ref[j] for j in range(heads)]
    for i in range(members):
        for j in range(heads):
            entry_ref[i * heads + j] = states[j]
        if i < members - 1:
            states = [advance((first_ref, second_ref)[j // per][i * per + j % per], states[j]) for j in range(heads)]


def spread(start, first, second):
    heads, size, _ = start.shape
    members = 2 * first.shape[0] // heads
    return pl.pallas_call(
        spread_kernel,
        in_specs=[IN_VMEM] * 3,
        out_specs=IN_VMEM,
        out_shape=jax.ShapeDtypeStruct((members * heads, size, size), F32),
        compiler_params=pltpu.CompilerParams(vmem_limit_bytes=SMALL),
        name="spread",
    )(*held_in_vmem(start, first, second))


def finish_kernel(lout_ref, cq_ref, states, gain_ref, out_ref):
    rights = [right3(state) for state in states]
    outs = [lout_ref[h] + mm3(left3(cq_ref[h]), right) for h, right in enumerate(rights)]
    roots = [jnp.sqrt(jnp.mean(out * out, axis=1, keepdims=True) + EPS) for out in outs]
    for h, (out, root) in enumerate(zip(outs, roots)):
        out_ref[:, head_cols(h)] = (out / root * gain_ref[:, head_cols(h)]).astype(BF16)


def finish(tokens, state, gain):
    (lout0, cq0), (lout1, cq1) = tokens
    count, size = lout0.shape[1], lout0.shape[2]
    groups, heads = 2, state.shape[0]
    per = 2
    step_heads = 4
    steps = heads // step_heads
    half = steps // groups

    def kernel(l0, c0, l1, c1, state_ref, gain_ref, out_ref):
        at = pl.program_id(0)

        def run(lout_ref, cq_ref, group):
            first = (at - group * half) * (step_heads // per)
            states = [state_ref[(first + h // per) * groups * per + group * per + h % per] for h in range(step_heads)]
            finish_kernel(lout_ref, cq_ref, states, gain_ref, out_ref)

        @pl.when(at < half)
        def _():
            run(l0, c0, 0)

        @pl.when(at >= half)
        def _():
            run(l1, c1, 1)

    low = pl.BlockSpec((step_heads, count, size), lambda g: (jnp.minimum(g, half - 1), 0, 0))
    high = pl.BlockSpec((step_heads, count, size), lambda g: (jnp.maximum(g - half, 0), 0, 0))
    return pl.pallas_call(
        kernel,
        grid=(steps,),
        in_specs=[
            low,
            low,
            high,
            high,
            IN_VMEM,
            pl.BlockSpec((1, step_heads * size), lambda g: (0, g)),
        ],
        out_specs=pl.BlockSpec((count, step_heads * size), lambda g: (0, g)),
        out_shape=jax.ShapeDtypeStruct((count, heads * size), BF16),
        compiler_params=pltpu.CompilerParams(vmem_limit_bytes=VMEM),
        name="finish",
    )(lout0, cq0, lout1, cq1, *held_in_vmem(state), gain.reshape(1, heads * size))


def local(queries, keys, values, beta_logit, gain):
    quad = lax.axis_size("zi")
    received = []
    saved = []
    for group in range(2):
        maps, inv, cross, scale = block_maps(group, keys, values, beta_logit)
        saved.append((inv, cross, scale))
        got = lax.all_to_all(maps, "zi", split_axis=0, concat_axis=0, tiled=True)
        received.append(got)
    tokens = [block_tokens(group, queries, keys, values, *saved[group]) for group in range(2)]
    totals = chain("quad_total", quad, received[1], chain("quad_total", quad, received[0]))
    quads = lax.all_to_all(totals, "zq", split_axis=0, concat_axis=0, tiled=True)
    whole = chain("group_total", lax.axis_size("zq"), quads)
    by_core = lax.all_gather(whole[0], "core")
    by_y = lax.all_gather(chain("chip_total", lax.axis_size("core"), by_core)[0], "y")
    by_x = lax.all_gather(chain("y_total", lax.axis_size("y"), by_y)[0], "x")
    place = jnp.stack([lax.axis_index("x"), lax.axis_index("y"), lax.axis_index("core")])
    starts = start_states(place, by_x, by_y, by_core, quads)
    mine = lax.all_to_all(starts, "zq", split_axis=0, concat_axis=0, tiled=True)
    entries = spread(mine, received[0], received[1])
    state = lax.all_to_all(entries, "zi", split_axis=0, concat_axis=0, tiled=True)
    return finish(tokens, state, gain)


def solution(mesh):
    fine = Mesh(mesh.devices.reshape(4, 4, 2, 4, 4), ("x", "y", "core", "zq", "zi"))
    every = ("x", "y", "core", "zq", "zi")
    return jax.shard_map(
        local,
        mesh=fine,
        in_specs=(
            P(every, None),
            P(every, None, None),
            P(every, None, None),
            P(None, None, every),
            P(),
        ),
        out_specs=P(every, None),
        check_vma=False,
    )
```

```python
import functools

import jax
import jax.numpy as jnp
from jax import lax
from jax.experimental import pallas as pl
from jax.experimental.pallas import tpu as pltpu
from jax.sharding import Mesh, PartitionSpec as P

F32 = jnp.float32
BF16 = jnp.bfloat16
BASE = 16
GROUP = 128 // BASE
EPS = 1e-06
VMEM = 58 * 1024 * 1024
SMALL = 16 * 1024 * 1024


def parts(x):
    hi = x.astype(BF16)
    lo = (x - hi.astype(F32)).astype(BF16)
    return hi, lo


def dot(a, b):
    return jnp.dot(a, b, preferred_element_type=F32)


def dot_nt(a, b):
    return lax.dot_general(a, b, (((1,), (1,)), ((), ())), preferred_element_type=F32)


def left3(x):
    hi, lo = parts(x)
    return jnp.concatenate([hi, lo], axis=1)


def right3(x):
    hi, lo = parts(x)
    row = jnp.concatenate([hi, lo], axis=1)
    return jnp.concatenate([row, row], axis=0)


def mm3(left, right):
    both = dot(left, right)
    half = both.shape[1] // 2
    return both[:, :half] + both[:, half:]


IN_VMEM = pl.BlockSpec(memory_space=pltpu.VMEM)


def held_in_vmem(*arrays):
    return [pltpu.with_memory_space_constraint(array, pltpu.VMEM) for array in arrays]


def iota(shape, dim):
    return lax.broadcasted_iota(jnp.int32, shape, dim)


def reciprocal_root(total):
    y = lax.rsqrt(total)
    return y * (1.5 - 0.5 * total * y * y)


def head_rows(ref, h):
    return ref[:, :, head_cols(h)].reshape(2 * ref.shape[0], 128)


def head_cols(h):
    return slice(h * 128, (h + 1) * 128)


def beta_rows_of(logits):
    heads, count = logits.shape[1], logits.shape[2]
    beta2 = 2.0 / (1.0 + jnp.exp(-logits))
    r_of = iota((count, 2 * count), 1)
    t_of = iota((count, 2 * count), 0)
    beta_rows = jnp.zeros((heads, 2 * count), F32)
    for j in range(2):
        pick = (r_of == 2 * t_of + j).astype(BF16)
        rest = beta2[j]
        for _ in range(3):
            piece = rest.astype(BF16)
            rest = rest - piece.astype(F32)
            beta_rows = beta_rows + dot(piece, pick)
    return beta_rows


def unit_keys(kb):
    kf = kb.astype(F32)
    return kf * reciprocal_root(jnp.sum(kf * kf, axis=1, keepdims=True) + EPS)


def solve_right(rhs, inv, cross):
    z2 = mm3(left3(rhs[:, 128:]), right3(inv[128:]))
    z1 = mm3(left3(rhs[:, :128] - mm3(left3(z2), right3(cross))), right3(inv[:128]))
    return jnp.concatenate([z1, z2], axis=1)


def through_rows(z, kb, vb):
    z_hi, z_lo = parts(z)
    k_hi, k_lo = parts(unit_keys(kb))
    both = jnp.concatenate([k_hi, vb], axis=1)
    prod = dot(z_hi, both) + dot(z_lo, both)
    return prod[:, :128] + dot(z_hi, k_lo), prod[:, 128:]


def maps_kernel(k_ref, v_ref, logit_ref, maps_ref, inv_ref, cross_ref, scale_ref, n_ref, r_ref, c_ref, t_ref, z_ref):
    rows = 2 * k_ref.shape[0]
    size = 128
    beta_rows = beta_rows_of(logit_ref[...])

    row256 = iota((rows, rows), 0)
    col256 = iota((rows, rows), 1)
    strict = row256 > col256
    diagonal = row256 == col256
    row128 = iota((size, size), 0)
    col128 = iota((size, size), 1)
    eye_b = (row128 == col128).astype(BF16)

    compact = [jnp.zeros((BASE, 128), F32) for _ in range(rows // BASE)]
    lane = iota((BASE, 128), 1)
    for h in range(GROUP):
        kb = head_rows(k_ref, h)
        grams = dot_nt(jnp.concatenate([kb, eye_b], axis=0), kb)
        gram = grams[:rows]
        kf = kb.astype(F32)
        n_col = reciprocal_root(jnp.sum(kf * kf, axis=1, keepdims=True) + EPS)
        n_row = reciprocal_root(jnp.sum(jnp.where(diagonal, gram, 0.0), axis=0, keepdims=True) + EPS)
        scale_row = n_row * beta_rows[h : h + 1, :]
        scale_ref[h : h + 1, :] = scale_row
        system = jnp.where(strict, gram, 0.0) * n_col * scale_row
        n_ref[h] = system
        cross_ref[h] = system[size:, :size]
        r_ref[h] = grams[rows:] * scale_row
        mine = (lane // BASE) == h
        for blk in range(rows // BASE):
            place = blk % GROUP
            tile = blk // GROUP
            slab = system[blk * BASE : (blk + 1) * BASE, tile * 128 : (tile + 1) * 128]
            shift = BASE * ((h - place) % GROUP)
            if shift:
                slab = pltpu.roll(slab, shift, axis=1)
            compact[blk] = jnp.where(mine, slab, compact[blk])

    identity = (iota((BASE, 128), 0) == (lane % BASE)).astype(F32)
    for blk in range(rows // BASE):
        below = compact[blk]
        inv = identity
        for step in range(BASE - 1):
            factor = jnp.take_along_axis(below, (lane // BASE) * BASE + step, axis=1, mode="promise_in_bounds")
            inv = inv - factor * inv[step : step + 1, :]
        c_ref[blk] = inv

    for h in range(GROUP):
        for tile in range(2):
            for place in range(GROUP):
                slab = c_ref[tile * GROUP + place]
                shift = BASE * ((place - h) % GROUP)
                if shift:
                    slab = pltpu.roll(slab, shift, axis=1)
                first = tile * 128 + place * BASE
                inv_ref[h, first : first + BASE] = jnp.where((lane // BASE) == place, slab, 0.0)
    width = BASE
    while width < size:
        odd = range(width, size, 2 * width)
        mask = col128[:width] // width
        for h in range(GROUP):
            for tile in range(2):
                base = tile * 128
                inv = inv_ref[h, base : base + 128]
                part = jnp.concatenate(
                    [
                        jnp.where(mask == at // width - 1, n_ref[h, base + at : base + at + width, base : base + 128], 0.0)
                        for at in odd
                    ],
                    axis=0,
                )
                t_ref[h, tile] = mm3(left3(part), right3(inv))
        for h in range(GROUP):
            for tile in range(2):
                base = tile * 128
                own = jnp.concatenate([inv_ref[h, base + at : base + at + width] for at in odd], axis=0)
                hi, lo = parts(t_ref[h, tile])
                both = jnp.concatenate([hi, lo], axis=1)
                none = jnp.zeros((width, 256), BF16)
                spread = []
                for i in range(len(odd)):
                    spread += [none, both[i * width : (i + 1) * width]]
                spread = jnp.concatenate(spread, axis=0)
                new = own - mm3(left3(own), jnp.concatenate([spread, spread], axis=0))
                for i, at in enumerate(odd):
                    inv_ref[h, base + at : base + at + width] = new[i * width : (i + 1) * width]
        width *= 2

    eye = (row128 == col128).astype(F32)
    for h in range(GROUP):
        z_ref[h, :, size:] = mm3(left3(r_ref[h, :, size:]), right3(inv_ref[h, size:]))
    for h in range(GROUP):
        r_ref[h, :, :size] = r_ref[h, :, :size] - mm3(left3(z_ref[h, :, size:]), right3(cross_ref[h]))
    for h in range(GROUP):
        z_ref[h, :, :size] = mm3(left3(r_ref[h, :, :size]), right3(inv_ref[h, :size]))
    for h in range(GROUP):
        through, fresh = through_rows(z_ref[h], head_rows(k_ref, h), head_rows(v_ref, h))
        maps_ref[h, :, :size] = eye - through
        maps_ref[h, :, size:] = fresh


def block_maps(group, keys, values, logits):
    rows = 2 * keys.shape[0]
    size = 128
    lanes = GROUP * size
    whole = lambda *shape: pl.BlockSpec(shape, lambda g: (0,) * len(shape))
    return pl.pallas_call(
        maps_kernel,
        grid=(1,),
        in_specs=[
            pl.BlockSpec((rows // 2, 2, lanes), lambda g: (0, 0, group)),
            pl.BlockSpec((rows // 2, 2, lanes), lambda g: (0, 0, group)),
            pl.BlockSpec((2, GROUP, rows // 2), lambda g: (0, group, 0)),
        ],
        out_specs=[
            whole(GROUP, size, 2 * size),
            whole(GROUP, rows, size),
            whole(GROUP, size, size),
            whole(GROUP, rows),
        ],
        out_shape=[
            jax.ShapeDtypeStruct((GROUP, size, 2 * size), F32),
            jax.ShapeDtypeStruct((GROUP, rows, size), F32),
            jax.ShapeDtypeStruct((GROUP, size, size), F32),
            jax.ShapeDtypeStruct((GROUP, rows), F32),
        ],
        scratch_shapes=[
            pltpu.VMEM((GROUP, rows, rows), F32),
            pltpu.VMEM((GROUP, size, rows), F32),
            pltpu.VMEM((rows // BASE, BASE, 128), F32),
            pltpu.VMEM((GROUP, 2, size // 2, size), F32),
            pltpu.VMEM((GROUP, size, rows), F32),
        ],
        compiler_params=pltpu.CompilerParams(vmem_limit_bytes=VMEM),
        name="block_maps",
    )(keys, values, logits)


def tokens_kernel(q_ref, k_ref, v_ref, inv_ref, cross_ref, scale_ref, lout_ref, cq_ref):
    count = q_ref.shape[0]
    seen = iota((count, 2 * count), 1) <= 2 * iota((count, 2 * count), 0) + 1
    for h in range(GROUP):
        kb = head_rows(k_ref, h)
        qb = q_ref[:, head_cols(h)]
        scores = jnp.where(seen, dot_nt(qb, kb), 0.0) * scale_ref[h : h + 1, :]
        z = solve_right(scores, inv_ref[h], cross_ref[h])
        through, fresh = through_rows(z, kb, head_rows(v_ref, h))
        qf = qb.astype(F32)
        nq = reciprocal_root(jnp.sum(qf * qf, axis=1, keepdims=True) + EPS)
        cq_ref[h] = nq * (qf - through)
        lout_ref[h] = nq * fresh


def block_tokens(group, queries, keys, values, inv, cross, scale):
    count, width = queries.shape
    rows = 2 * count
    size = 128
    lanes = GROUP * size
    whole = lambda *shape: pl.BlockSpec(shape, lambda g: (0,) * len(shape))
    return pl.pallas_call(
        tokens_kernel,
        grid=(1,),
        in_specs=[
            pl.BlockSpec((count, lanes), lambda g: (0, group)),
            pl.BlockSpec((rows // 2, 2, lanes), lambda g: (0, 0, group)),
            pl.BlockSpec((rows // 2, 2, lanes), lambda g: (0, 0, group)),
            whole(GROUP, rows, size),
            whole(GROUP, size, size),
            whole(GROUP, rows),
        ],
        out_specs=[whole(GROUP, count, size), whole(GROUP, count, size)],
        out_shape=[
            jax.ShapeDtypeStruct((GROUP, count, size), F32),
            jax.ShapeDtypeStruct((GROUP, count, size), F32),
        ],
        compiler_params=pltpu.CompilerParams(vmem_limit_bytes=VMEM),
        name="block_tokens",
    )(queries, keys, values, inv, cross, scale)


def times_map(piece, acc):
    left = left3(piece[:, :128])
    hi, lo = parts(acc)
    return dot(left, jnp.concatenate([hi, hi], axis=0)) + dot(left[:, :128], lo)


def after(piece, acc):
    size = piece.shape[0]
    moved = times_map(piece, acc)
    return jnp.concatenate([moved[:, :size], moved[:, size:] + piece[:, size:]], axis=1)


def advance(piece, state):
    return times_map(piece, state) + piece[:, piece.shape[0] :]


def chain_kernel(pieces, maps_ref, *refs):
    total_ref = refs[-1]
    heads = maps_ref.shape[0] // pieces
    done = 0
    for earlier in refs[:-1]:
        done = earlier.shape[0]
        total_ref[:done] = earlier[...]
    accs = [maps_ref[j] for j in range(heads)]
    for i in range(1, pieces):
        accs = [after(maps_ref[i * heads + j], acc) for j, acc in enumerate(accs)]
    for j, acc in enumerate(accs):
        total_ref[done + j] = acc


def chain(name, pieces, maps, *earlier):
    count = maps.shape[0] // pieces + sum(part.shape[0] for part in earlier)
    return pl.pallas_call(
        functools.partial(chain_kernel, pieces),
        in_specs=[IN_VMEM] * (1 + len(earlier)),
        out_specs=IN_VMEM,
        out_shape=jax.ShapeDtypeStruct((count,) + maps.shape[1:], F32),
        compiler_params=pltpu.CompilerParams(vmem_limit_bytes=SMALL),
        name=name,
    )(*held_in_vmem(maps, *earlier))


def send_kernel(place_ref, maps_ref, earlier_ref, own_ref, right_ref, left_ref):
    size = maps_ref.shape[1]
    early = earlier_ref.shape[0]
    per = early
    pieces = maps_ref.shape[0] // per
    accs = [maps_ref[j] for j in range(per)]
    for i in range(1, pieces):
        accs = [after(maps_ref[i * per + j], acc) for j, acc in enumerate(accs)]
    totals = [earlier_ref[j] for j in range(early)] + accs
    me = place_ref[3]

    def pick(ahead):
        at = lax.rem(me + ahead, len(totals))
        found = totals[0]
        for j in range(1, len(totals)):
            found = jnp.where(at == j, totals[j], found)
        return found

    own_ref[...] = pick(0)
    ahead, opposite, behind = pick(1), pick(2), pick(3)
    right_ref[0] = ahead[:, :size]
    right_ref[1] = ahead[:, size:]
    right_ref[2] = opposite[:, :size]
    left_ref[0] = behind[:, :size]
    left_ref[1] = behind[:, size:]
    left_ref[2] = opposite[:, size:]


def quad_sends(place, maps, earlier):
    size, wide = maps.shape[1:]
    return pl.pallas_call(
        send_kernel,
        in_specs=[pl.BlockSpec(memory_space=pltpu.SMEM)] + [IN_VMEM] * 2,
        out_specs=[IN_VMEM] * 3,
        out_shape=[
            jax.ShapeDtypeStruct((size, wide), F32),
            jax.ShapeDtypeStruct((3, size, size), F32),
            jax.ShapeDtypeStruct((3, size, size), F32),
        ],
        compiler_params=pltpu.CompilerParams(vmem_limit_bytes=SMALL),
        name="quad_sends",
    )(place, *held_in_vmem(maps, earlier))


def gather_kernel(place_ref, own_ref, near_left_ref, near_right_ref, far_a_ref, far_b_ref, quads_ref, total_ref):
    size = own_ref.shape[0]
    count = quads_ref.shape[0]
    me = place_ref[3]
    quads_ref[me] = own_ref[...]
    for ahead, first, second in (
        (1, near_right_ref[0], near_right_ref[1]),
        (2, far_a_ref[...], far_b_ref[...]),
        (3, near_left_ref[0], near_left_ref[1]),
    ):
        at = lax.rem(me + ahead, count)
        quads_ref[at, :, :size] = first
        quads_ref[at, :, size:] = second
    acc = quads_ref[0]
    for i in range(1, count):
        acc = after(quads_ref[i], acc)
    total_ref[...] = acc


def gather_quads(place, own, near_left, near_right, far_a, far_b):
    size, wide = own.shape
    return pl.pallas_call(
        gather_kernel,
        in_specs=[pl.BlockSpec(memory_space=pltpu.SMEM)] + [IN_VMEM] * 5,
        out_specs=[IN_VMEM] * 2,
        out_shape=[
            jax.ShapeDtypeStruct((4, size, wide), F32),
            jax.ShapeDtypeStruct((size, wide), F32),
        ],
        compiler_params=pltpu.CompilerParams(vmem_limit_bytes=SMALL),
        name="gather_quads",
    )(place, *held_in_vmem(own, near_left, near_right, far_a, far_b))


def start_kernel(place_ref, by_x_ref, by_y_ref, by_core_ref, quads_ref, entry_ref):
    size = by_x_ref.shape[1]
    state = jnp.zeros((size, size), F32)
    for axis, ref in enumerate((by_x_ref, by_y_ref, by_core_ref)):
        state = lax.fori_loop(0, place_ref[axis], lambda i, s, ref=ref: advance(ref[i], s), state)
    entry_ref[0] = state
    for i in range(quads_ref.shape[0] - 1):
        state = advance(quads_ref[i], state)
        entry_ref[i + 1] = state


def start_states(place, by_x, by_y, by_core, quads):
    count, size, _ = quads.shape
    return pl.pallas_call(
        start_kernel,
        in_specs=[pl.BlockSpec(memory_space=pltpu.SMEM)] + [IN_VMEM] * 4,
        out_specs=IN_VMEM,
        out_shape=jax.ShapeDtypeStruct((count, size, size), F32),
        compiler_params=pltpu.CompilerParams(vmem_limit_bytes=SMALL),
        name="start_states",
    )(place, *held_in_vmem(by_x, by_y, by_core, quads))


def spread_kernel(start_ref, first_ref, second_ref, entry_ref):
    heads = start_ref.shape[0]
    per = heads // 2
    members = first_ref.shape[0] // per
    states = [start_ref[j] for j in range(heads)]
    for i in range(members):
        for j in range(heads):
            entry_ref[i * heads + j] = states[j]
        if i < members - 1:
            states = [advance((first_ref, second_ref)[j // per][i * per + j % per], states[j]) for j in range(heads)]


def spread(start, first, second):
    heads, size, _ = start.shape
    members = 2 * first.shape[0] // heads
    return pl.pallas_call(
        spread_kernel,
        in_specs=[IN_VMEM] * 3,
        out_specs=IN_VMEM,
        out_shape=jax.ShapeDtypeStruct((members * heads, size, size), F32),
        compiler_params=pltpu.CompilerParams(vmem_limit_bytes=SMALL),
        name="spread",
    )(*held_in_vmem(start, first, second))


def finish_kernel(lout_ref, cq_ref, states, gain_ref, out_ref):
    rights = [right3(state) for state in states]
    outs = [lout_ref[h] + mm3(left3(cq_ref[h]), right) for h, right in enumerate(rights)]
    roots = [jnp.sqrt(jnp.mean(out * out, axis=1, keepdims=True) + EPS) for out in outs]
    for h, (out, root) in enumerate(zip(outs, roots)):
        out_ref[:, head_cols(h)] = (out / root * gain_ref[:, head_cols(h)]).astype(BF16)


def finish(tokens, state, gain):
    (lout0, cq0), (lout1, cq1) = tokens
    count, size = lout0.shape[1], lout0.shape[2]
    groups, heads = 2, state.shape[0]
    per = 2
    step_heads = 4
    steps = heads // step_heads
    half = steps // groups

    def kernel(l0, c0, l1, c1, state_ref, gain_ref, out_ref):
        at = pl.program_id(0)

        def run(lout_ref, cq_ref, group):
            first = (at - group * half) * (step_heads // per)
            states = [state_ref[(first + h // per) * groups * per + group * per + h % per] for h in range(step_heads)]
            finish_kernel(lout_ref, cq_ref, states, gain_ref, out_ref)

        @pl.when(at < half)
        def _():
            run(l0, c0, 0)

        @pl.when(at >= half)
        def _():
            run(l1, c1, 1)

    low = pl.BlockSpec((step_heads, count, size), lambda g: (jnp.minimum(g, half - 1), 0, 0))
    high = pl.BlockSpec((step_heads, count, size), lambda g: (jnp.maximum(g - half, 0), 0, 0))
    return pl.pallas_call(
        kernel,
        grid=(steps,),
        in_specs=[
            low,
            low,
            high,
            high,
            IN_VMEM,
            pl.BlockSpec((1, step_heads * size), lambda g: (0, g)),
        ],
        out_specs=pl.BlockSpec((count, step_heads * size), lambda g: (0, g)),
        out_shape=jax.ShapeDtypeStruct((count, heads * size), BF16),
        compiler_params=pltpu.CompilerParams(vmem_limit_bytes=VMEM),
        name="finish",
    )(lout0, cq0, lout1, cq1, *held_in_vmem(state), gain.reshape(1, heads * size))


def local(queries, keys, values, beta_logit, gain):
    quad = lax.axis_size("zi")
    received = []
    saved = []
    for group in range(2):
        maps, inv, cross, scale = block_maps(group, keys, values, beta_logit)
        saved.append((inv, cross, scale))
        got = lax.all_to_all(maps, "zi", split_axis=0, concat_axis=0, tiled=True)
        received.append(got)
    tokens = [block_tokens(group, queries, keys, values, *saved[group]) for group in range(2)]
    place = jnp.stack([lax.axis_index(axis) for axis in ("x", "y", "core", "zq")])
    ring = lax.axis_size("zq")
    rightward = [(i, (i + 1) % ring) for i in range(ring)]
    leftward = [(i, (i - 1) % ring) for i in range(ring)]
    own, to_right, to_left = quad_sends(place, received[1], chain("quad_total", quad, received[0]))
    from_left = lax.ppermute(to_right, "zq", rightward)
    from_right = lax.ppermute(to_left, "zq", leftward)
    far_a = lax.ppermute(from_left[2], "zq", rightward)
    far_b = lax.ppermute(from_right[2], "zq", leftward)
    quads, whole = gather_quads(place, own, from_left, from_right, far_a, far_b)
    by_core = lax.all_gather(whole, "core")
    by_y = lax.all_gather(chain("chip_total", lax.axis_size("core"), by_core)[0], "y")
    by_x = lax.all_gather(chain("y_total", lax.axis_size("y"), by_y)[0], "x")
    starts = start_states(place, by_x, by_y, by_core, quads)
    mine = lax.all_to_all(starts, "zq", split_axis=0, concat_axis=0, tiled=True)
    entries = spread(mine, received[0], received[1])
    state = lax.all_to_all(entries, "zi", split_axis=0, concat_axis=0, tiled=True)
    return finish(tokens, state, gain)


def solution(mesh):
    fine = Mesh(mesh.devices.reshape(4, 4, 2, 4, 4), ("x", "y", "core", "zq", "zi"))
    every = ("x", "y", "core", "zq", "zi")
    return jax.shard_map(
        local,
        mesh=fine,
        in_specs=(
            P(every, None),
            P(every, None, None),
            P(every, None, None),
            P(None, None, every),
            P(),
        ),
        out_specs=P(every, None),
        check_vma=False,
    )
```

```python
import functools

import jax
import jax.numpy as jnp
from jax import lax
from jax.experimental import pallas as pl
from jax.experimental.pallas import tpu as pltpu
from jax.sharding import Mesh, PartitionSpec as P

F32 = jnp.float32
BF16 = jnp.bfloat16
BASE = 16
GROUP = 128 // BASE
EPS = 1e-06
VMEM = 58 * 1024 * 1024
SMALL = 16 * 1024 * 1024


def parts(x):
    hi = x.astype(BF16)
    lo = (x - hi.astype(F32)).astype(BF16)
    return hi, lo


def dot(a, b):
    return jnp.dot(a, b, preferred_element_type=F32)


def dot_nt(a, b):
    return lax.dot_general(a, b, (((1,), (1,)), ((), ())), preferred_element_type=F32)


def left3(x):
    hi, lo = parts(x)
    return jnp.concatenate([hi, lo], axis=1)


def right3(x):
    hi, lo = parts(x)
    row = jnp.concatenate([hi, lo], axis=1)
    return jnp.concatenate([row, row], axis=0)


def mm3(left, right):
    both = dot(left, right)
    half = both.shape[1] // 2
    return both[:, :half] + both[:, half:]


IN_VMEM = pl.BlockSpec(memory_space=pltpu.VMEM)


def held_in_vmem(*arrays):
    return [pltpu.with_memory_space_constraint(array, pltpu.VMEM) for array in arrays]


def iota(shape, dim):
    return lax.broadcasted_iota(jnp.int32, shape, dim)


def reciprocal_root(total):
    y = lax.rsqrt(total)
    return y * (1.5 - 0.5 * total * y * y)


def head_rows(ref, h):
    return ref[:, :, head_cols(h)].reshape(2 * ref.shape[0], 128)


def head_cols(h):
    return slice(h * 128, (h + 1) * 128)


def beta_rows_of(logits):
    heads, count = logits.shape[1], logits.shape[2]
    beta2 = 2.0 / (1.0 + jnp.exp(-logits))
    r_of = iota((count, 2 * count), 1)
    t_of = iota((count, 2 * count), 0)
    beta_rows = jnp.zeros((heads, 2 * count), F32)
    for j in range(2):
        pick = (r_of == 2 * t_of + j).astype(BF16)
        rest = beta2[j]
        for _ in range(3):
            piece = rest.astype(BF16)
            rest = rest - piece.astype(F32)
            beta_rows = beta_rows + dot(piece, pick)
    return beta_rows


def unit_keys(kb):
    kf = kb.astype(F32)
    return kf * reciprocal_root(jnp.sum(kf * kf, axis=1, keepdims=True) + EPS)


def solve_right(rhs, inv, cross):
    z2 = mm3(left3(rhs[:, 128:]), right3(inv[128:]))
    z1 = mm3(left3(rhs[:, :128] - mm3(left3(z2), right3(cross))), right3(inv[:128]))
    return jnp.concatenate([z1, z2], axis=1)


def through_rows(z, kb, vb):
    z_hi, z_lo = parts(z)
    k_hi, k_lo = parts(unit_keys(kb))
    both = jnp.concatenate([k_hi, vb], axis=1)
    prod = dot(z_hi, both) + dot(z_lo, both)
    return prod[:, :128] + dot(z_hi, k_lo), prod[:, 128:]


def maps_kernel(k_ref, v_ref, logit_ref, maps_ref, inv_ref, cross_ref, scale_ref, n_ref, r_ref, c_ref, t_ref, z_ref):
    rows = 2 * k_ref.shape[0]
    size = 128
    beta_rows = beta_rows_of(logit_ref[...])

    row256 = iota((rows, rows), 0)
    col256 = iota((rows, rows), 1)
    strict = row256 > col256
    diagonal = row256 == col256
    row128 = iota((size, size), 0)
    col128 = iota((size, size), 1)
    eye_b = (row128 == col128).astype(BF16)

    compact = [jnp.zeros((BASE, 128), F32) for _ in range(rows // BASE)]
    lane = iota((BASE, 128), 1)
    for h in range(GROUP):
        kb = head_rows(k_ref, h)
        grams = dot_nt(jnp.concatenate([kb, eye_b], axis=0), kb)
        gram = grams[:rows]
        kf = kb.astype(F32)
        n_col = reciprocal_root(jnp.sum(kf * kf, axis=1, keepdims=True) + EPS)
        n_row = reciprocal_root(jnp.sum(jnp.where(diagonal, gram, 0.0), axis=0, keepdims=True) + EPS)
        scale_row = n_row * beta_rows[h : h + 1, :]
        scale_ref[h : h + 1, :] = scale_row
        system = jnp.where(strict, gram, 0.0) * n_col * scale_row
        n_ref[h] = system
        cross_ref[h] = system[size:, :size]
        r_ref[h] = grams[rows:] * scale_row
        mine = (lane // BASE) == h
        for blk in range(rows // BASE):
            place = blk % GROUP
            tile = blk // GROUP
            slab = system[blk * BASE : (blk + 1) * BASE, tile * 128 : (tile + 1) * 128]
            shift = BASE * ((h - place) % GROUP)
            if shift:
                slab = pltpu.roll(slab, shift, axis=1)
            compact[blk] = jnp.where(mine, slab, compact[blk])

    identity = (iota((BASE, 128), 0) == (lane % BASE)).astype(F32)
    for blk in range(rows // BASE):
        below = compact[blk]
        inv = identity
        for step in range(BASE - 1):
            factor = jnp.take_along_axis(below, (lane // BASE) * BASE + step, axis=1, mode="promise_in_bounds")
            inv = inv - factor * inv[step : step + 1, :]
        c_ref[blk] = inv

    for h in range(GROUP):
        for tile in range(2):
            for place in range(GROUP):
                slab = c_ref[tile * GROUP + place]
                shift = BASE * ((place - h) % GROUP)
                if shift:
                    slab = pltpu.roll(slab, shift, axis=1)
                first = tile * 128 + place * BASE
                inv_ref[h, first : first + BASE] = jnp.where((lane // BASE) == place, slab, 0.0)
    width = BASE
    while width < size:
        odd = range(width, size, 2 * width)
        mask = col128[:width] // width
        for h in range(GROUP):
            for tile in range(2):
                base = tile * 128
                inv = inv_ref[h, base : base + 128]
                part = jnp.concatenate(
                    [
                        jnp.where(mask == at // width - 1, n_ref[h, base + at : base + at + width, base : base + 128], 0.0)
                        for at in odd
                    ],
                    axis=0,
                )
                t_ref[h, tile] = mm3(left3(part), right3(inv))
        for h in range(GROUP):
            for tile in range(2):
                base = tile * 128
                own = jnp.concatenate([inv_ref[h, base + at : base + at + width] for at in odd], axis=0)
                hi, lo = parts(t_ref[h, tile])
                both = jnp.concatenate([hi, lo], axis=1)
                none = jnp.zeros((width, 256), BF16)
                spread = []
                for i in range(len(odd)):
                    spread += [none, both[i * width : (i + 1) * width]]
                spread = jnp.concatenate(spread, axis=0)
                new = own - mm3(left3(own), jnp.concatenate([spread, spread], axis=0))
                for i, at in enumerate(odd):
                    inv_ref[h, base + at : base + at + width] = new[i * width : (i + 1) * width]
        width *= 2

    eye = (row128 == col128).astype(F32)
    for h in range(GROUP):
        z_ref[h, :, size:] = mm3(left3(r_ref[h, :, size:]), right3(inv_ref[h, size:]))
    for h in range(GROUP):
        r_ref[h, :, :size] = r_ref[h, :, :size] - mm3(left3(z_ref[h, :, size:]), right3(cross_ref[h]))
    for h in range(GROUP):
        z_ref[h, :, :size] = mm3(left3(r_ref[h, :, :size]), right3(inv_ref[h, :size]))
    for h in range(GROUP):
        through, fresh = through_rows(z_ref[h], head_rows(k_ref, h), head_rows(v_ref, h))
        maps_ref[h, :, :size] = eye - through
        maps_ref[h, :, size:] = fresh


def block_maps(group, keys, values, logits):
    rows = 2 * keys.shape[0]
    size = 128
    lanes = GROUP * size
    whole = lambda *shape: pl.BlockSpec(shape, lambda g: (0,) * len(shape))
    return pl.pallas_call(
        maps_kernel,
        grid=(1,),
        in_specs=[
            pl.BlockSpec((rows // 2, 2, lanes), lambda g: (0, 0, group)),
            pl.BlockSpec((rows // 2, 2, lanes), lambda g: (0, 0, group)),
            pl.BlockSpec((2, GROUP, rows // 2), lambda g: (0, group, 0)),
        ],
        out_specs=[
            whole(GROUP, size, 2 * size),
            whole(GROUP, rows, size),
            whole(GROUP, size, size),
            whole(GROUP, rows),
        ],
        out_shape=[
            jax.ShapeDtypeStruct((GROUP, size, 2 * size), F32),
            jax.ShapeDtypeStruct((GROUP, rows, size), F32),
            jax.ShapeDtypeStruct((GROUP, size, size), F32),
            jax.ShapeDtypeStruct((GROUP, rows), F32),
        ],
        scratch_shapes=[
            pltpu.VMEM((GROUP, rows, rows), F32),
            pltpu.VMEM((GROUP, size, rows), F32),
            pltpu.VMEM((rows // BASE, BASE, 128), F32),
            pltpu.VMEM((GROUP, 2, size // 2, size), F32),
            pltpu.VMEM((GROUP, size, rows), F32),
        ],
        compiler_params=pltpu.CompilerParams(vmem_limit_bytes=VMEM),
        name="block_maps",
    )(keys, values, logits)


def tokens_kernel(q_ref, k_ref, v_ref, inv_ref, cross_ref, scale_ref, lout_ref, cq_ref):
    count = q_ref.shape[0]
    seen = iota((count, 2 * count), 1) <= 2 * iota((count, 2 * count), 0) + 1
    for h in range(GROUP):
        kb = head_rows(k_ref, h)
        qb = q_ref[:, head_cols(h)]
        scores = jnp.where(seen, dot_nt(qb, kb), 0.0) * scale_ref[h : h + 1, :]
        z = solve_right(scores, inv_ref[h], cross_ref[h])
        through, fresh = through_rows(z, kb, head_rows(v_ref, h))
        qf = qb.astype(F32)
        nq = reciprocal_root(jnp.sum(qf * qf, axis=1, keepdims=True) + EPS)
        cq_ref[h] = nq * (qf - through)
        lout_ref[h] = nq * fresh


def block_tokens(group, queries, keys, values, inv, cross, scale):
    count, width = queries.shape
    rows = 2 * count
    size = 128
    lanes = GROUP * size
    whole = lambda *shape: pl.BlockSpec(shape, lambda g: (0,) * len(shape))
    return pl.pallas_call(
        tokens_kernel,
        grid=(1,),
        in_specs=[
            pl.BlockSpec((count, lanes), lambda g: (0, group)),
            pl.BlockSpec((rows // 2, 2, lanes), lambda g: (0, 0, group)),
            pl.BlockSpec((rows // 2, 2, lanes), lambda g: (0, 0, group)),
            whole(GROUP, rows, size),
            whole(GROUP, size, size),
            whole(GROUP, rows),
        ],
        out_specs=[whole(GROUP, count, size), whole(GROUP, count, size)],
        out_shape=[
            jax.ShapeDtypeStruct((GROUP, count, size), F32),
            jax.ShapeDtypeStruct((GROUP, count, size), F32),
        ],
        compiler_params=pltpu.CompilerParams(vmem_limit_bytes=VMEM),
        name="block_tokens",
    )(queries, keys, values, inv, cross, scale)


def times_map(piece, acc):
    left = left3(piece[:, :128])
    hi, lo = parts(acc)
    return dot(left, jnp.concatenate([hi, hi], axis=0)) + dot(left[:, :128], lo)


def after(piece, acc):
    size = piece.shape[0]
    moved = times_map(piece, acc)
    return jnp.concatenate([moved[:, :size], moved[:, size:] + piece[:, size:]], axis=1)


def advance(piece, state):
    return times_map(piece, state) + piece[:, piece.shape[0] :]


def placed_chain_kernel(pieces, place_ref, maps_ref, total_ref, placed_ref):
    for axis in range(place_ref.shape[0]):
        placed_ref[axis] = place_ref[axis]
    chain_kernel(pieces, maps_ref, total_ref)


def placed_chain(name, pieces, maps, place):
    smem = pl.BlockSpec(memory_space=pltpu.SMEM)
    return pl.pallas_call(
        functools.partial(placed_chain_kernel, pieces),
        in_specs=[smem, IN_VMEM],
        out_specs=[IN_VMEM, smem],
        out_shape=[
            jax.ShapeDtypeStruct((maps.shape[0] // pieces,) + maps.shape[1:], F32),
            jax.ShapeDtypeStruct(place.shape, place.dtype),
        ],
        compiler_params=pltpu.CompilerParams(vmem_limit_bytes=SMALL),
        name=name,
    )(place, *held_in_vmem(maps))


def chain_kernel(pieces, maps_ref, *refs):
    total_ref = refs[-1]
    heads = maps_ref.shape[0] // pieces
    done = 0
    for earlier in refs[:-1]:
        done = earlier.shape[0]
        total_ref[:done] = earlier[...]
    accs = [maps_ref[j] for j in range(heads)]
    for i in range(1, pieces):
        accs = [after(maps_ref[i * heads + j], acc) for j, acc in enumerate(accs)]
    for j, acc in enumerate(accs):
        total_ref[done + j] = acc


def chain(name, pieces, maps, *earlier):
    count = maps.shape[0] // pieces + sum(part.shape[0] for part in earlier)
    return pl.pallas_call(
        functools.partial(chain_kernel, pieces),
        in_specs=[IN_VMEM] * (1 + len(earlier)),
        out_specs=IN_VMEM,
        out_shape=jax.ShapeDtypeStruct((count,) + maps.shape[1:], F32),
        compiler_params=pltpu.CompilerParams(vmem_limit_bytes=SMALL),
        name=name,
    )(*held_in_vmem(maps, *earlier))


def start_kernel(place_ref, by_x_ref, by_y_ref, by_core_ref, quads_ref, entry_ref):
    size = by_x_ref.shape[1]
    state = jnp.zeros((size, size), F32)
    for axis, ref in enumerate((by_x_ref, by_y_ref, by_core_ref)):
        state = lax.fori_loop(0, place_ref[axis], lambda i, s, ref=ref: advance(ref[i], s), state)
    entry_ref[0] = state
    for i in range(quads_ref.shape[0] - 1):
        state = advance(quads_ref[i], state)
        entry_ref[i + 1] = state


def start_states(place, by_x, by_y, by_core, quads):
    count, size, _ = quads.shape
    return pl.pallas_call(
        start_kernel,
        in_specs=[pl.BlockSpec(memory_space=pltpu.SMEM)] + [IN_VMEM] * 4,
        out_specs=IN_VMEM,
        out_shape=jax.ShapeDtypeStruct((count, size, size), F32),
        compiler_params=pltpu.CompilerParams(vmem_limit_bytes=SMALL),
        name="start_states",
    )(place, *held_in_vmem(by_x, by_y, by_core, quads))


def spread_kernel(start_ref, first_ref, second_ref, entry_ref):
    heads = start_ref.shape[0]
    per = heads // 2
    members = first_ref.shape[0] // per
    states = [start_ref[j] for j in range(heads)]
    for i in range(members):
        for j in range(heads):
            entry_ref[i * heads + j] = states[j]
        if i < members - 1:
            states = [advance((first_ref, second_ref)[j // per][i * per + j % per], states[j]) for j in range(heads)]


def spread(start, first, second):
    heads, size, _ = start.shape
    members = 2 * first.shape[0] // heads
    return pl.pallas_call(
        spread_kernel,
        in_specs=[IN_VMEM] * 3,
        out_specs=IN_VMEM,
        out_shape=jax.ShapeDtypeStruct((members * heads, size, size), F32),
        compiler_params=pltpu.CompilerParams(vmem_limit_bytes=SMALL),
        name="spread",
    )(*held_in_vmem(start, first, second))


def finish_kernel(lout_ref, cq_ref, states, gain_ref, out_ref):
    rights = [right3(state) for state in states]
    outs = [lout_ref[h] + mm3(left3(cq_ref[h]), right) for h, right in enumerate(rights)]
    roots = [jnp.sqrt(jnp.mean(out * out, axis=1, keepdims=True) + EPS) for out in outs]
    for h, (out, root) in enumerate(zip(outs, roots)):
        out_ref[:, head_cols(h)] = (out / root * gain_ref[:, head_cols(h)]).astype(BF16)


def finish(tokens, state, gain):
    (lout0, cq0), (lout1, cq1) = tokens
    count, size = lout0.shape[1], lout0.shape[2]
    groups, heads = 2, state.shape[0]
    per = 2
    step_heads = 4
    steps = heads // step_heads
    half = steps // groups

    def kernel(l0, c0, l1, c1, state_ref, gain_ref, out_ref):
        at = pl.program_id(0)

        def run(lout_ref, cq_ref, group):
            first = (at - group * half) * (step_heads // per)
            states = [state_ref[(first + h // per) * groups * per + group * per + h % per] for h in range(step_heads)]
            finish_kernel(lout_ref, cq_ref, states, gain_ref, out_ref)

        @pl.when(at < half)
        def _():
            run(l0, c0, 0)

        @pl.when(at >= half)
        def _():
            run(l1, c1, 1)

    low = pl.BlockSpec((step_heads, count, size), lambda g: (jnp.minimum(g, half - 1), 0, 0))
    high = pl.BlockSpec((step_heads, count, size), lambda g: (jnp.maximum(g - half, 0), 0, 0))
    return pl.pallas_call(
        kernel,
        grid=(steps,),
        in_specs=[
            low,
            low,
            high,
            high,
            IN_VMEM,
            pl.BlockSpec((1, step_heads * size), lambda g: (0, g)),
        ],
        out_specs=pl.BlockSpec((count, step_heads * size), lambda g: (0, g)),
        out_shape=jax.ShapeDtypeStruct((count, heads * size), BF16),
        compiler_params=pltpu.CompilerParams(vmem_limit_bytes=VMEM),
        name="finish",
    )(lout0, cq0, lout1, cq1, *held_in_vmem(state), gain.reshape(1, heads * size))


def local(queries, keys, values, beta_logit, gain):
    quad = lax.axis_size("zi")
    received = []
    saved = []
    for group in range(2):
        maps, inv, cross, scale = block_maps(group, keys, values, beta_logit)
        saved.append((inv, cross, scale))
        got = lax.all_to_all(maps, "zi", split_axis=0, concat_axis=0, tiled=True)
        received.append(got)
    tokens = [block_tokens(group, queries, keys, values, *saved[group]) for group in range(2)]
    place = jnp.stack([lax.axis_index("x"), lax.axis_index("y"), lax.axis_index("core")])
    early, place = placed_chain("quad_total", quad, received[0], place)
    totals = chain("quad_total", quad, received[1], early)
    quads = lax.all_to_all(totals, "zq", split_axis=0, concat_axis=0, tiled=True)
    whole = chain("group_total", lax.axis_size("zq"), quads)
    by_core = lax.all_gather(whole[0], "core")
    by_y = lax.all_gather(chain("chip_total", lax.axis_size("core"), by_core)[0], "y")
    by_x = lax.all_gather(chain("y_total", lax.axis_size("y"), by_y)[0], "x")
    starts = start_states(place, by_x, by_y, by_core, quads)
    mine = lax.all_to_all(starts, "zq", split_axis=0, concat_axis=0, tiled=True)
    entries = spread(mine, received[0], received[1])
    state = lax.all_to_all(entries, "zi", split_axis=0, concat_axis=0, tiled=True)
    return finish(tokens, state, gain)


def solution(mesh):
    fine = Mesh(mesh.devices.reshape(4, 4, 2, 4, 4), ("x", "y", "core", "zq", "zi"))
    every = ("x", "y", "core", "zq", "zi")
    return jax.shard_map(
        local,
        mesh=fine,
        in_specs=(
            P(every, None),
            P(every, None, None),
            P(every, None, None),
            P(None, None, every),
            P(),
        ),
        out_specs=P(every, None),
        check_vma=False,
    )
```

```python
import functools

import jax
import jax.numpy as jnp
from jax import lax
from jax.experimental import pallas as pl
from jax.experimental.pallas import tpu as pltpu
from jax.sharding import Mesh, PartitionSpec as P

F32 = jnp.float32
BF16 = jnp.bfloat16
BASE = 16
GROUP = 128 // BASE
EPS = 1e-06
VMEM = 58 * 1024 * 1024
SMALL = 16 * 1024 * 1024


def parts(x):
    hi = x.astype(BF16)
    lo = (x - hi.astype(F32)).astype(BF16)
    return hi, lo


def dot(a, b):
    return jnp.dot(a, b, preferred_element_type=F32)


def dot_nt(a, b):
    return lax.dot_general(a, b, (((1,), (1,)), ((), ())), preferred_element_type=F32)


def left3(x):
    hi, lo = parts(x)
    return jnp.concatenate([hi, lo], axis=1)


def right3(x):
    hi, lo = parts(x)
    row = jnp.concatenate([hi, lo], axis=1)
    return jnp.concatenate([row, row], axis=0)


def mm3(left, right):
    both = dot(left, right)
    half = both.shape[1] // 2
    return both[:, :half] + both[:, half:]


IN_VMEM = pl.BlockSpec(memory_space=pltpu.VMEM)


def held_in_vmem(*arrays):
    return [pltpu.with_memory_space_constraint(array, pltpu.VMEM) for array in arrays]


def iota(shape, dim):
    return lax.broadcasted_iota(jnp.int32, shape, dim)


def reciprocal_root(total):
    y = lax.rsqrt(total)
    return y * (1.5 - 0.5 * total * y * y)


def head_rows(ref, h):
    return ref[:, :, head_cols(h)].reshape(2 * ref.shape[0], 128)


def head_cols(h):
    return slice(h * 128, (h + 1) * 128)


def beta_rows_of(logits):
    heads, count = logits.shape[1], logits.shape[2]
    beta2 = 2.0 / (1.0 + jnp.exp(-logits))
    r_of = iota((count, 2 * count), 1)
    t_of = iota((count, 2 * count), 0)
    beta_rows = jnp.zeros((heads, 2 * count), F32)
    for j in range(2):
        pick = (r_of == 2 * t_of + j).astype(BF16)
        rest = beta2[j]
        for _ in range(3):
            piece = rest.astype(BF16)
            rest = rest - piece.astype(F32)
            beta_rows = beta_rows + dot(piece, pick)
    return beta_rows


def unit_keys(kb):
    kf = kb.astype(F32)
    return kf * reciprocal_root(jnp.sum(kf * kf, axis=1, keepdims=True) + EPS)


def solve_right(rhs, inv, cross):
    z2 = mm3(left3(rhs[:, 128:]), right3(inv[128:]))
    z1 = mm3(left3(rhs[:, :128] - mm3(left3(z2), right3(cross))), right3(inv[:128]))
    return jnp.concatenate([z1, z2], axis=1)


def through_rows(z, kb, vb):
    z_hi, z_lo = parts(z)
    k_hi, k_lo = parts(unit_keys(kb))
    both = jnp.concatenate([k_hi, vb], axis=1)
    prod = dot(z_hi, both) + dot(z_lo, both)
    return prod[:, :128] + dot(z_hi, k_lo), prod[:, 128:]


def maps_kernel(k_ref, v_ref, logit_ref, maps_ref, inv_ref, cross_ref, scale_ref, n_ref, r_ref, c_ref, t_ref, z_ref):
    rows = 2 * k_ref.shape[0]
    size = 128
    beta_rows = beta_rows_of(logit_ref[...])

    row256 = iota((rows, rows), 0)
    col256 = iota((rows, rows), 1)
    strict = row256 > col256
    diagonal = row256 == col256
    row128 = iota((size, size), 0)
    col128 = iota((size, size), 1)
    eye_b = (row128 == col128).astype(BF16)

    compact = [jnp.zeros((BASE, 128), F32) for _ in range(rows // BASE)]
    lane = iota((BASE, 128), 1)
    for h in range(GROUP):
        kb = head_rows(k_ref, h)
        grams = dot_nt(jnp.concatenate([kb, eye_b], axis=0), kb)
        gram = grams[:rows]
        kf = kb.astype(F32)
        n_col = reciprocal_root(jnp.sum(kf * kf, axis=1, keepdims=True) + EPS)
        n_row = reciprocal_root(jnp.sum(jnp.where(diagonal, gram, 0.0), axis=0, keepdims=True) + EPS)
        scale_row = n_row * beta_rows[h : h + 1, :]
        scale_ref[h : h + 1, :] = scale_row
        system = jnp.where(strict, gram, 0.0) * n_col * scale_row
        n_ref[h] = system
        cross_ref[h] = system[size:, :size]
        r_ref[h] = grams[rows:] * scale_row
        mine = (lane // BASE) == h
        for blk in range(rows // BASE):
            place = blk % GROUP
            tile = blk // GROUP
            slab = system[blk * BASE : (blk + 1) * BASE, tile * 128 : (tile + 1) * 128]
            shift = BASE * ((h - place) % GROUP)
            if shift:
                slab = pltpu.roll(slab, shift, axis=1)
            compact[blk] = jnp.where(mine, slab, compact[blk])

    identity = (iota((BASE, 128), 0) == (lane % BASE)).astype(F32)
    for blk in range(rows // BASE):
        below = compact[blk]
        inv = identity
        for step in range(BASE - 1):
            factor = jnp.take_along_axis(below, (lane // BASE) * BASE + step, axis=1, mode="promise_in_bounds")
            inv = inv - factor * inv[step : step + 1, :]
        c_ref[blk] = inv

    for h in range(GROUP):
        for tile in range(2):
            for place in range(GROUP):
                slab = c_ref[tile * GROUP + place]
                shift = BASE * ((place - h) % GROUP)
                if shift:
                    slab = pltpu.roll(slab, shift, axis=1)
                first = tile * 128 + place * BASE
                inv_ref[h, first : first + BASE] = jnp.where((lane // BASE) == place, slab, 0.0)
    width = BASE
    while width < size:
        odd = range(width, size, 2 * width)
        mask = col128[:width] // width
        for h in range(GROUP):
            for tile in range(2):
                base = tile * 128
                inv = inv_ref[h, base : base + 128]
                part = jnp.concatenate(
                    [
                        jnp.where(mask == at // width - 1, n_ref[h, base + at : base + at + width, base : base + 128], 0.0)
                        for at in odd
                    ],
                    axis=0,
                )
                t_ref[h, tile] = mm3(left3(part), right3(inv))
        for h in range(GROUP):
            for tile in range(2):
                base = tile * 128
                own = jnp.concatenate([inv_ref[h, base + at : base + at + width] for at in odd], axis=0)
                hi, lo = parts(t_ref[h, tile])
                both = jnp.concatenate([hi, lo], axis=1)
                none = jnp.zeros((width, 256), BF16)
                spread = []
                for i in range(len(odd)):
                    spread += [none, both[i * width : (i + 1) * width]]
                spread = jnp.concatenate(spread, axis=0)
                new = own - mm3(left3(own), jnp.concatenate([spread, spread], axis=0))
                for i, at in enumerate(odd):
                    inv_ref[h, base + at : base + at + width] = new[i * width : (i + 1) * width]
        width *= 2

    eye = (row128 == col128).astype(F32)
    for h in range(GROUP):
        z_ref[h, :, size:] = mm3(left3(r_ref[h, :, size:]), right3(inv_ref[h, size:]))
    for h in range(GROUP):
        r_ref[h, :, :size] = r_ref[h, :, :size] - mm3(left3(z_ref[h, :, size:]), right3(cross_ref[h]))
    for h in range(GROUP):
        z_ref[h, :, :size] = mm3(left3(r_ref[h, :, :size]), right3(inv_ref[h, :size]))
    for h in range(GROUP):
        through, fresh = through_rows(z_ref[h], head_rows(k_ref, h), head_rows(v_ref, h))
        maps_ref[h, :, :size] = eye - through
        maps_ref[h, :, size:] = fresh


def block_maps(group, keys, values, logits):
    rows = 2 * keys.shape[0]
    size = 128
    lanes = GROUP * size
    whole = lambda *shape: pl.BlockSpec(shape, lambda g: (0,) * len(shape))
    return pl.pallas_call(
        maps_kernel,
        grid=(1,),
        in_specs=[
            pl.BlockSpec((rows // 2, 2, lanes), lambda g: (0, 0, group)),
            pl.BlockSpec((rows // 2, 2, lanes), lambda g: (0, 0, group)),
            pl.BlockSpec((2, GROUP, rows // 2), lambda g: (0, group, 0)),
        ],
        out_specs=[
            whole(GROUP, size, 2 * size),
            whole(GROUP, rows, size),
            whole(GROUP, size, size),
            whole(GROUP, rows),
        ],
        out_shape=[
            jax.ShapeDtypeStruct((GROUP, size, 2 * size), F32),
            jax.ShapeDtypeStruct((GROUP, rows, size), F32),
            jax.ShapeDtypeStruct((GROUP, size, size), F32),
            jax.ShapeDtypeStruct((GROUP, rows), F32),
        ],
        scratch_shapes=[
            pltpu.VMEM((GROUP, rows, rows), F32),
            pltpu.VMEM((GROUP, size, rows), F32),
            pltpu.VMEM((rows // BASE, BASE, 128), F32),
            pltpu.VMEM((GROUP, 2, size // 2, size), F32),
            pltpu.VMEM((GROUP, size, rows), F32),
        ],
        compiler_params=pltpu.CompilerParams(vmem_limit_bytes=VMEM),
        name="block_maps",
    )(keys, values, logits)


def tokens_kernel(q_ref, k_ref, v_ref, inv_ref, cross_ref, scale_ref, lout_ref, cq_ref):
    count = q_ref.shape[0]
    seen = iota((count, 2 * count), 1) <= 2 * iota((count, 2 * count), 0) + 1
    for h in range(GROUP):
        kb = head_rows(k_ref, h)
        qb = q_ref[:, head_cols(h)]
        scores = jnp.where(seen, dot_nt(qb, kb), 0.0) * scale_ref[h : h + 1, :]
        z = solve_right(scores, inv_ref[h], cross_ref[h])
        through, fresh = through_rows(z, kb, head_rows(v_ref, h))
        qf = qb.astype(F32)
        nq = reciprocal_root(jnp.sum(qf * qf, axis=1, keepdims=True) + EPS)
        cq_ref[h] = nq * (qf - through)
        lout_ref[h] = nq * fresh


def block_tokens(group, queries, keys, values, inv, cross, scale):
    count, width = queries.shape
    rows = 2 * count
    size = 128
    lanes = GROUP * size
    whole = lambda *shape: pl.BlockSpec(shape, lambda g: (0,) * len(shape))
    return pl.pallas_call(
        tokens_kernel,
        grid=(1,),
        in_specs=[
            pl.BlockSpec((count, lanes), lambda g: (0, group)),
            pl.BlockSpec((rows // 2, 2, lanes), lambda g: (0, 0, group)),
            pl.BlockSpec((rows // 2, 2, lanes), lambda g: (0, 0, group)),
            whole(GROUP, rows, size),
            whole(GROUP, size, size),
            whole(GROUP, rows),
        ],
        out_specs=[whole(GROUP, count, size), whole(GROUP, count, size)],
        out_shape=[
            jax.ShapeDtypeStruct((GROUP, count, size), F32),
            jax.ShapeDtypeStruct((GROUP, count, size), F32),
        ],
        compiler_params=pltpu.CompilerParams(vmem_limit_bytes=VMEM),
        name="block_tokens",
    )(queries, keys, values, inv, cross, scale)


def times_map(piece, acc):
    left = left3(piece[:, :128])
    hi, lo = parts(acc)
    return dot(left, jnp.concatenate([hi, hi], axis=0)) + dot(left[:, :128], lo)


def after(piece, acc):
    size = piece.shape[0]
    moved = times_map(piece, acc)
    return jnp.concatenate([moved[:, :size], moved[:, size:] + piece[:, size:]], axis=1)


def advance(piece, state):
    return times_map(piece, state) + piece[:, piece.shape[0] :]


def chain_kernel(pieces, maps_ref, *refs):
    total_ref = refs[-1]
    heads = maps_ref.shape[0] // pieces
    done = 0
    for earlier in refs[:-1]:
        done = earlier.shape[0]
        total_ref[:done] = earlier[...]
    accs = [maps_ref[j] for j in range(heads)]
    for i in range(1, pieces):
        accs = [after(maps_ref[i * heads + j], acc) for j, acc in enumerate(accs)]
    for j, acc in enumerate(accs):
        total_ref[done + j] = acc


def chain(name, pieces, maps, *earlier):
    count = maps.shape[0] // pieces + sum(part.shape[0] for part in earlier)
    return pl.pallas_call(
        functools.partial(chain_kernel, pieces),
        in_specs=[IN_VMEM] * (1 + len(earlier)),
        out_specs=IN_VMEM,
        out_shape=jax.ShapeDtypeStruct((count,) + maps.shape[1:], F32),
        compiler_params=pltpu.CompilerParams(vmem_limit_bytes=SMALL),
        name=name,
    )(*held_in_vmem(maps, *earlier))


def copies_kernel(core_ref, by_core_ref, copies_ref):
    size = by_core_ref.shape[1]
    chip = after(by_core_ref[1], by_core_ref[0])
    half = jnp.where(core_ref[0] == 0, chip[:, :size], chip[:, size:])
    for i in range(copies_ref.shape[0]):
        copies_ref[i] = half


def chip_copies(core, by_core, chips):
    size = by_core.shape[1]
    return pl.pallas_call(
        copies_kernel,
        in_specs=[pl.BlockSpec(memory_space=pltpu.SMEM), IN_VMEM],
        out_specs=IN_VMEM,
        out_shape=jax.ShapeDtypeStruct((chips, size, size), F32),
        compiler_params=pltpu.CompilerParams(vmem_limit_bytes=SMALL),
        name="chip_copies",
    )(core, *held_in_vmem(by_core))


def start_kernel(place_ref, mine_ref, other_ref, by_core_ref, quads_ref, entry_ref):
    size = mine_ref.shape[1]
    first = place_ref[1] == 0

    def by_chip(i, state):
        mine, other = mine_ref[i], other_ref[i]
        transition = jnp.where(first, mine, other)
        offset = jnp.where(first, other, mine)
        return times_map(transition, state) + offset

    state = lax.fori_loop(0, place_ref[0], by_chip, jnp.zeros((size, size), F32))
    state = jnp.where(first, state, advance(by_core_ref[0], state))
    entry_ref[0] = state
    for i in range(quads_ref.shape[0] - 1):
        state = advance(quads_ref[i], state)
        entry_ref[i + 1] = state


def start_states(place, mine, other, by_core, quads):
    count, size, _ = quads.shape
    return pl.pallas_call(
        start_kernel,
        in_specs=[pl.BlockSpec(memory_space=pltpu.SMEM)] + [IN_VMEM] * 4,
        out_specs=IN_VMEM,
        out_shape=jax.ShapeDtypeStruct((count, size, size), F32),
        compiler_params=pltpu.CompilerParams(vmem_limit_bytes=SMALL),
        name="start_states",
    )(place, *held_in_vmem(mine, other, by_core, quads))


def spread_kernel(start_ref, first_ref, second_ref, entry_ref):
    heads = start_ref.shape[0]
    per = heads // 2
    members = first_ref.shape[0] // per
    states = [start_ref[j] for j in range(heads)]
    for i in range(members):
        for j in range(heads):
            entry_ref[i * heads + j] = states[j]
        if i < members - 1:
            states = [advance((first_ref, second_ref)[j // per][i * per + j % per], states[j]) for j in range(heads)]


def spread(start, first, second):
    heads, size, _ = start.shape
    members = 2 * first.shape[0] // heads
    return pl.pallas_call(
        spread_kernel,
        in_specs=[IN_VMEM] * 3,
        out_specs=IN_VMEM,
        out_shape=jax.ShapeDtypeStruct((members * heads, size, size), F32),
        compiler_params=pltpu.CompilerParams(vmem_limit_bytes=SMALL),
        name="spread",
    )(*held_in_vmem(start, first, second))


def finish_kernel(lout_ref, cq_ref, states, gain_ref, out_ref):
    rights = [right3(state) for state in states]
    outs = [lout_ref[h] + mm3(left3(cq_ref[h]), right) for h, right in enumerate(rights)]
    roots = [jnp.sqrt(jnp.mean(out * out, axis=1, keepdims=True) + EPS) for out in outs]
    for h, (out, root) in enumerate(zip(outs, roots)):
        out_ref[:, head_cols(h)] = (out / root * gain_ref[:, head_cols(h)]).astype(BF16)


def finish(tokens, state, gain):
    (lout0, cq0), (lout1, cq1) = tokens
    count, size = lout0.shape[1], lout0.shape[2]
    groups, heads = 2, state.shape[0]
    per = 2
    step_heads = 4
    steps = heads // step_heads
    half = steps // groups

    def kernel(l0, c0, l1, c1, state_ref, gain_ref, out_ref):
        at = pl.program_id(0)

        def run(lout_ref, cq_ref, group):
            first = (at - group * half) * (step_heads // per)
            states = [state_ref[(first + h // per) * groups * per + group * per + h % per] for h in range(step_heads)]
            finish_kernel(lout_ref, cq_ref, states, gain_ref, out_ref)

        @pl.when(at < half)
        def _():
            run(l0, c0, 0)

        @pl.when(at >= half)
        def _():
            run(l1, c1, 1)

    low = pl.BlockSpec((step_heads, count, size), lambda g: (jnp.minimum(g, half - 1), 0, 0))
    high = pl.BlockSpec((step_heads, count, size), lambda g: (jnp.maximum(g - half, 0), 0, 0))
    return pl.pallas_call(
        kernel,
        grid=(steps,),
        in_specs=[
            low,
            low,
            high,
            high,
            IN_VMEM,
            pl.BlockSpec((1, step_heads * size), lambda g: (0, g)),
        ],
        out_specs=pl.BlockSpec((count, step_heads * size), lambda g: (0, g)),
        out_shape=jax.ShapeDtypeStruct((count, heads * size), BF16),
        compiler_params=pltpu.CompilerParams(vmem_limit_bytes=VMEM),
        name="finish",
    )(lout0, cq0, lout1, cq1, *held_in_vmem(state), gain.reshape(1, heads * size))


def local(queries, keys, values, beta_logit, gain):
    quad = lax.axis_size("zi")
    received = []
    saved = []
    for group in range(2):
        maps, inv, cross, scale = block_maps(group, keys, values, beta_logit)
        saved.append((inv, cross, scale))
        got = lax.all_to_all(maps, "zi", split_axis=0, concat_axis=0, tiled=True)
        received.append(got)
    tokens = [block_tokens(group, queries, keys, values, *saved[group]) for group in range(2)]
    totals = chain("quad_total", quad, received[1], chain("quad_total", quad, received[0]))
    quads = lax.all_to_all(totals, "zq", split_axis=0, concat_axis=0, tiled=True)
    whole = chain("group_total", lax.axis_size("zq"), quads)
    by_core = lax.all_gather(whole[0], "core")
    core = lax.axis_index("core")
    chips = lax.axis_size("x") * lax.axis_size("y")
    copies = chip_copies(core.reshape(1), by_core, chips)
    mine = lax.all_to_all(copies, ("x", "y"), split_axis=0, concat_axis=0, tiled=True)
    other = lax.ppermute(mine, "core", [(0, 1), (1, 0)])
    place = jnp.stack([lax.axis_index(("x", "y")), core])
    starts = start_states(place, mine, other, by_core, quads)
    held = lax.all_to_all(starts, "zq", split_axis=0, concat_axis=0, tiled=True)
    entries = spread(held, received[0], received[1])
    state = lax.all_to_all(entries, "zi", split_axis=0, concat_axis=0, tiled=True)
    return finish(tokens, state, gain)


def solution(mesh):
    fine = Mesh(mesh.devices.reshape(4, 4, 2, 4, 4), ("x", "y", "core", "zq", "zi"))
    every = ("x", "y", "core", "zq", "zi")
    return jax.shard_map(
        local,
        mesh=fine,
        in_specs=(
            P(every, None),
            P(every, None, None),
            P(every, None, None),
            P(None, None, every),
            P(),
        ),
        out_specs=P(every, None),
        check_vma=False,
    )
```
